128 devices in a mesh: fsdp: 16 (over z_lo, x, core), tp: 8 (over y, z_hi).
Axes of the slice: x: 4, y: 4, z: 4 (z_hi: 2, z_lo: 2; z = z_hi * 2 + z_lo), core: 2. Of those that a mesh axis runs over, the one named last changes fastest.
Arguments:
- activations: bfloat16 [16384, 4096], P('fsdp', 'tp'), may hold values from -6 to 6
- cotangent: bfloat16 [16384, 4096], P('fsdp', 'tp'), may hold values from -6 to 6
- step_count: int32 [1], replicated, may hold values from 1 to 8
- region_of: int32 [16], replicated, may hold values from 0 to 3, never falling along the last dimension, each value on 1 to 8 neighbouring positions
- weight_master: float32 [4096, 4096], P('fsdp', 'tp'), may hold values from -0.75 to 0.75
- weight_moment: float32 [4096, 4096], P('fsdp', 'tp'), may hold values from -1.5 to 1.5
- weight_second: float32 [4096, 4096], P('fsdp', 'tp'), may hold values from 0.01 to 1
- adapter_copy: bfloat16 [2, 4, 4096, 256], P(None, None, 'tp'), may hold values from -6 to 6
- adapter_master: float32 [2, 4, 4096, 256], P(None, None, ('tp', 'fsdp')), may hold values from -0.75 to 0.75
- adapter_moment: float32 [2, 4, 4096, 256], P(None, None, ('tp', 'fsdp')), may hold values from -1.5 to 1.5
- adapter_second: float32 [2, 4, 4096, 256], P(None, None, ('tp', 'fsdp')), may hold values from 0.01 to 1
Outputs:
- new_weight: float32 [4096, 4096], P('fsdp', 'tp')
- new_weight_moment: float32 [4096, 4096], P('fsdp', 'tp')
- new_weight_second: float32 [4096, 4096], P('fsdp', 'tp')
- weight_next: bfloat16 [4096, 4096], P(None, 'tp')
- new_adapter: float32 [2, 4, 4096, 256], P(None, None, ('tp', 'fsdp'))
- new_adapter_moment: float32 [2, 4, 4096, 256], P(None, None, ('tp', 'fsdp'))
- new_adapter_second: float32 [2, 4, 4096, 256], P(None, None, ('tp', 'fsdp'))
- adapter_next: bfloat16 [2, 4, 4096, 256], P(None, None, 'tp')
The draws below stay inside these ranges and needn't reach their ends.
Inputs may be any that keep to these rules, and one draw needn't show every extreme that they name: Never falling along the fsdp indices; region_of is nondecreasing; each of the 4 regions holds 1 to 8 consecutive fsdp indices, and one region holds exactly 8.
All inputs are finite; a program needn't handle non-finite values.
Results may differ from the reference program's by a relative error of at most 0.0049.
Values may be sent and summed in bfloat16 or wider, within the bound.
No kernel may reach another device: no remote copies, remote signals or barrier semaphores. Data moves between devices by JAX's collectives and lax.ppermute only.
A program may use at most 128 MiB of HBM per device.

```python
import math
import jax
import jax.numpy as jnp
import numpy as np
from jax import lax

D = 4096
R = 256
REGIONS = 4
TOK_DEV = 1024
TOKENS = 16384
N_FSDP = 16


def raised(result, own_key, source, target, blocks, factor):
    def block_of(position):
        return (jnp.arange(result.shape[position]) // (result.shape[position] // blocks)).reshape((-1,) + (1,) * (result.ndim - 1 - position))

    one_side = jax.random.permutation(own_key, blocks)[block_of(target)]
    far = (block_of(target) + blocks // 2) % blocks
    return jnp.where((block_of(source) == one_side) | (block_of(source) == far), factor * result, result)


def block_levels(stream_key, extent, split, least, largest):
    gain = 1.0
    for dim, parts in split:
        steps = jax.random.uniform(jax.random.fold_in(jax.random.fold_in(stream_key, 6), dim), (parts,), jnp.float32, least / len(split), largest / len(split))
        gain = gain * jnp.repeat(jnp.exp(steps), extent[dim] // parts).reshape((-1,) + (1,) * (len(extent) - 1 - dim))
    return gain


def profile(amount, total, bound, slope):
    loads = [(1 << 20) // math.isqrt(rank ** slope) + 1 for rank in range(2, amount + 1)]
    rest, given = total - bound - (amount - 1), [1] * (amount - 1)
    while rest > 0:
        candidates = [i for i in range(amount - 1) if given[i] < bound]
        pool, budget = sum([loads[i] for i in candidates]), rest
        for i in candidates:
            more = min(bound - given[i], max(1, budget * loads[i] // pool), rest)
            given[i] = given[i] + more
            rest = rest - more
    return np.array([bound] + given)


def ragged(key, count, total, reach, skew):
    if count == 2:
        one = jax.random.randint(key, (), max(1, total - reach), min(reach, total - 1) + 1)
        return jnp.stack([one, total - one])
    lengths = jnp.asarray(profile(count, total, reach, skew), jnp.int32)
    couples = (count - 1) // 2
    source_of, receiver = lengths[1:1 + 2 * couples:2], lengths[2:2 + 2 * couples:2]
    slack = jnp.minimum(source_of - 1, reach - receiver)
    moved = jax.random.randint(jax.random.fold_in(key, 1), (couples,), 0, 1 << 20) % (slack + 1)
    lengths = lengths.at[1:1 + 2 * couples:2].set(source_of - moved).at[2:2 + 2 * couples:2].set(receiver + moved)
    return lengths[jax.random.permutation(jax.random.fold_in(key, 2), count)]


def noise(stream_key, extent, width, limit, pieces=(), held_as=jnp.bfloat16):
    result = width * jax.random.normal(stream_key, extent, jnp.float32)
    if pieces:
        result = result * block_levels(stream_key, extent, pieces, -0.22, 0.18)
    return jnp.clip(result, -limit, limit).astype(held_as)


def noise_with(own_key, extent, scale, most, shards, heavy, held_as=jnp.bfloat16):
    array = scale * jax.random.normal(own_key, extent, jnp.float32)
    if shards:
        array = array * block_levels(own_key, extent, shards, -0.22, 0.18)
    return jnp.clip(raised(array, jax.random.fold_in(own_key, 3), *heavy), -most, most).astype(held_as)


def setup_inputs(seed: int = 0) -> dict:
    splits = jax.random.split(jax.random.key(seed), 12)
    activations = noise_with(splits[0], (TOKENS, D), 1.0, 6.0, ((0, 16), (1, 8)), (0, 1, 16, 2.0))
    cotangent = noise(splits[1], (TOKENS, D), 1.0, 6.0, ((0, 16), (1, 8)))
    step_count = jax.random.randint(splits[2], (1,), 1, 9).astype(jnp.int32)
    region_of = jnp.searchsorted(jnp.cumsum(ragged(splits[3], REGIONS, N_FSDP, N_FSDP // 2, 1)), jnp.arange(N_FSDP), side="right").astype(jnp.int32)
    weight_master = noise(splits[4], (D, D), 0.05, 0.75, ((0, 16), (1, 8)), jnp.float32)
    weight_moment = noise(splits[5], (D, D), 0.1, 1.5, ((0, 16), (1, 8)), jnp.float32)
    weight_second = jnp.clip(jnp.exp(math.log(1.0) - 4.6051702 * jax.random.uniform(splits[6], (D, D), jnp.float32) ** block_levels(splits[6], (D, D), ((0, 16), (1, 8)), -0.2, 0.2)), 0.01, 1.0)
    adapter_copy = noise(splits[7], (2, REGIONS, D, R), 1.0, 6.0, ((2, 8),))
    adapter_master = noise(splits[8], (2, REGIONS, D, R), 0.05, 0.75, ((2, 128),), jnp.float32)
    adapter_moment = noise(splits[9], (2, REGIONS, D, R), 0.1, 1.5, ((2, 128),), jnp.float32)
    adapter_second = jnp.clip(jnp.exp(math.log(1.0) - 4.6051702 * jax.random.uniform(splits[10], (2, REGIONS, D, R), jnp.float32) ** block_levels(splits[10], (2, REGIONS, D, R), ((2, 128),), -0.2, 0.2)), 0.01, 1.0)
    return dict(activations=activations, cotangent=cotangent, step_count=step_count, region_of=region_of, weight_master=weight_master, weight_moment=weight_moment, weight_second=weight_second, adapter_copy=adapter_copy, adapter_master=adapter_master, adapter_moment=adapter_moment, adapter_second=adapter_second)


beta_first = 0.9
beta_second = 0.95
adam_eps = 1e-08
learn_rate = 0.1
decay_rate = 0.1

def adamw_update(param, moment, second, grad, step_count):
    step_float = step_count[0].astype(jnp.float32)
    first_fix = 1.0 - jnp.power(jnp.float32(beta_first), step_float)
    second_fix = 1.0 - jnp.power(jnp.float32(beta_second), step_float)
    moment_new = beta_first * moment + (1.0 - beta_first) * grad
    second_new = beta_second * second + (1.0 - beta_second) * grad * grad
    ratio = moment_new / first_fix / (jnp.sqrt(second_new / second_fix) + adam_eps)
    param_new = param - learn_rate * (ratio + decay_rate * param)
    return (param_new, moment_new, second_new)

def contract_rows(left, right):
    return lax.dot_general(left, right, (((0,), (0,)), ((), ())), preferred_element_type=jnp.float32)

def reference(activations, cotangent, step_count, region_of, weight_master, weight_moment, weight_second, adapter_copy, adapter_master, adapter_moment, adapter_second):
    grad_scale = math.sqrt(D / TOKENS)
    inv_width = 1.0 / math.sqrt(D)
    inv_rank = 1.0 / math.sqrt(R)
    grad_weight = contract_rows(activations, cotangent) * (inv_width * grad_scale)

    def add_block(block, accum):
        first_row = (block * TOK_DEV).astype(jnp.int32)
        act_block = lax.dynamic_slice_in_dim(activations, first_row, TOK_DEV, 0)
        cot_block = lax.dynamic_slice_in_dim(cotangent, first_row, TOK_DEV, 0)
        region = region_of[block]
        chosen = lax.dynamic_index_in_dim(adapter_copy, region, 1, keepdims=False)
        low_down = (jnp.dot(act_block, chosen[0], preferred_element_type=jnp.float32) * inv_width).astype(jnp.bfloat16)
        low_up = (jnp.dot(cot_block, chosen[1], preferred_element_type=jnp.float32) * inv_rank).astype(jnp.bfloat16)
        grad_down = contract_rows(act_block, low_up) * (inv_width * grad_scale)
        grad_up = contract_rows(cot_block, low_down) * (inv_rank * grad_scale)
        partial_grad = jnp.stack([grad_down, grad_up])
        region_hot = (jnp.arange(REGIONS, dtype=jnp.int32) == region).astype(jnp.float32)
        return accum + region_hot[None, :, None, None] * partial_grad[:, None]
    grad_adapter = lax.fori_loop(0, N_FSDP, add_block, jnp.zeros((2, REGIONS, D, R), jnp.float32))
    new_weight, new_weight_moment, new_weight_second = adamw_update(weight_master, weight_moment, weight_second, grad_weight, step_count)
    new_adapter, new_adapter_moment, new_adapter_second = adamw_update(adapter_master, adapter_moment, adapter_second, grad_adapter, step_count)
    return (new_weight, new_weight_moment, new_weight_second, new_weight.astype(jnp.bfloat16), new_adapter, new_adapter_moment, new_adapter_second, new_adapter.astype(jnp.bfloat16))
```

```python
import math

import jax
import jax.numpy as jnp
from jax import lax
from jax.sharding import PartitionSpec as P

beta_first = 0.9
beta_second = 0.95
adam_eps = 1e-08
learn_rate = 0.1
decay_rate = 0.1

AXES = ("fsdp", "tp")
F32 = jnp.float32
BF16 = jnp.bfloat16


def adamw_update(param, moment, second, grad, step_count):
    step_float = step_count[0].astype(jnp.float32)
    first_fix = 1.0 - jnp.power(jnp.float32(beta_first), step_float)
    second_fix = 1.0 - jnp.power(jnp.float32(beta_second), step_float)
    moment_new = beta_first * moment + (1.0 - beta_first) * grad
    second_new = beta_second * second + (1.0 - beta_second) * grad * grad
    ratio = moment_new / first_fix / (jnp.sqrt(second_new / second_fix) + adam_eps)
    param_new = param - learn_rate * (ratio + decay_rate * param)
    return (param_new, moment_new, second_new)


def contract_rows(left, right):
    return lax.dot_general(
        left, right, (((0,), (0,)), ((), ())), preferred_element_type=jnp.float32
    )


def device_number(x, y, zl, zh, c):
    return (zl * 8 + x * 2 + c) * 8 + (y * 2 + zh)


def move(array, where):
    pairs = []
    for x in range(4):
        for y in range(4):
            for zl in range(2):
                for zh in range(2):
                    for c in range(2):
                        a, b, d, e, g = where(x, y, zl, zh, c)
                        pairs.append(
                            (device_number(x, y, zl, zh, c), device_number(a % 4, b % 4, d, e, g))
                        )
    return lax.ppermute(array, AXES, pairs)


def along_x(k):
    return lambda x, y, zl, zh, c: (x + k, y, zl, zh, c)


def along_y(k):
    return lambda x, y, zl, zh, c: (x, y + k, zl, zh, c)


def other_core(x, y, zl, zh, c):
    return (x, y, zl, zh, 1 - c)


def other_zl(x, y, zl, zh, c):
    return (x, y, 1 - zl, zh, c)


def other_zh(x, y, zl, zh, c):
    return (x, y, zl, 1 - zh, c)


def to_owner(ka, kb):
    return lambda x, y, zl, zh, c: (2 * ((x & 1) ^ ka) + zh, y, zl ^ kb, x >> 1, c)


def shards(
    activations,
    cotangent,
    step_count,
    region_of,
    weight_master,
    weight_moment,
    weight_second,
    adapter_copy,
    adapter_master,
    adapter_moment,
    adapter_second,
):
    fsdp_count = lax.axis_size("fsdp")
    tp_count = lax.axis_size("tp")
    tok_dev = activations.shape[0]
    width = activations.shape[1] * tp_count
    rank = adapter_copy.shape[3]
    region_count = adapter_copy.shape[1]
    grad_scale = math.sqrt(width / (tok_dev * fsdp_count))
    inv_width = 1.0 / math.sqrt(width)
    inv_rank = 1.0 / math.sqrt(rank)
    f = lax.axis_index("fsdp")
    t = lax.axis_index("tp")
    zl, x, c = f // 8, (f // 2) % 4, f % 2
    y, zh = t // 2, t % 2

    index_hot = (jnp.arange(fsdp_count, dtype=jnp.int32) == f).astype(jnp.int32)
    own_region = jnp.sum(index_hot * region_of)
    chosen = lax.dynamic_index_in_dim(adapter_copy, own_region, 1, keepdims=False)
    down_part = jnp.dot(activations, chosen[0], preferred_element_type=F32) * inv_width
    up_part = jnp.dot(cotangent, chosen[1], preferred_element_type=F32) * inv_rank
    low_part = jnp.concatenate([down_part.astype(BF16), up_part.astype(BF16)], axis=1)
    quarter = tok_dev // 4

    def low_for(k):
        return lax.dynamic_slice_in_dim(low_part, ((y + k) % 4) * quarter, quarter, 0)

    low_sum = low_for(0).astype(F32)
    for k in (1, 3, 2):
        low_sum = low_sum + move(low_for(k), along_y(k)).astype(F32)
    low_sum = low_sum.astype(BF16)
    low_own = (low_sum.astype(F32) + move(low_sum, other_zh).astype(F32)).astype(BF16)
    low = jnp.zeros((tok_dev, 2 * rank), BF16)
    low = lax.dynamic_update_slice_in_dim(low, low_own, y * quarter, 0)
    for k in (1, 3, 2):
        low = lax.dynamic_update_slice_in_dim(
            low, move(low_own, along_y(k)), ((y - k) % 4) * quarter, 0
        )
    low_down, low_up = low[:, :rank], low[:, rank:]
    grad_down = contract_rows(activations, low_up) * (inv_width * grad_scale)
    grad_up = contract_rows(cotangent, low_down) * (inv_rank * grad_scale)
    partial_grad = jnp.stack([grad_down, grad_up]).astype(BF16)
    rows = partial_grad.shape[1] // fsdp_count
    parts = partial_grad.reshape(2, fsdp_count, rows, rank)
    got = lax.all_to_all(parts, "fsdp", 1, 0, tiled=False)
    region_hot = (region_of[None, :] == jnp.arange(region_count)[:, None]).astype(BF16)
    grad_adapter = lax.dot_general(
        region_hot, got.reshape(fsdp_count, 2 * rows * rank), (((1,), (0,)), ((), ())),
        preferred_element_type=F32,
    ).reshape(region_count, 2, rows, rank).transpose(1, 0, 2, 3)
    new_adapter, new_adapter_moment, new_adapter_second = adamw_update(
        adapter_master, adapter_moment, adapter_second, grad_adapter, step_count
    )
    adapter_next = lax.all_gather(new_adapter.astype(BF16), "fsdp", axis=2, tiled=True)

    half = activations.shape[1] // 2
    act_own = lax.dynamic_slice_in_dim(activations, c * half, half, 1)
    act_other = move(lax.dynamic_slice_in_dim(activations, (1 - c) * half, half, 1), other_core)
    act = jnp.concatenate([act_own, act_other], axis=0)
    act_back = move(act, along_y(1))
    act_ahead = move(act, along_y(-1))
    act_far = jnp.concatenate(
        [move(act_back[:tok_dev], along_y(1)), move(act_ahead[tok_dev:], along_y(-1))], axis=0
    )
    cot_own = jnp.concatenate([cotangent, move(cotangent, other_core)], axis=0)
    cot_zh = move(cotangent, other_zh)
    cot_zh = jnp.concatenate([cot_zh, move(cot_zh, other_core)], axis=0)

    def partial(left):
        both = [contract_rows(left, cot_own), contract_rows(left, cot_zh)]
        return (jnp.concatenate(both, axis=1) * (inv_width * grad_scale)).astype(BF16)

    def sum_over_x(part):
        wide = part.shape[1] // 4

        def piece(k):
            q = (x + k) % 4
            start = ((q // 2) ^ zh) * (2 * wide) + (q % 2) * wide
            return lax.dynamic_slice_in_dim(part, start, wide, 1)

        total = piece(0).astype(F32)
        for k in (1, 3, 2):
            total = total + move(piece(k), along_x(k)).astype(F32)
        return total.astype(BF16)

    near = sum_over_x(
        jnp.concatenate([partial(act), partial(act_ahead), partial(act_back)], axis=0)
    )
    far = sum_over_x(partial(act_far))
    blocks = jnp.concatenate([near, far], axis=0).reshape(4, half, half)
    place = jnp.array([0, 1, 3, 2], jnp.int32)
    sums = []
    for ka in range(2):
        total = None
        for kb in range(2):
            row_y = 2 * (zl ^ kb) + ((x & 1) ^ ka)
            block = lax.dynamic_index_in_dim(blocks, place[(row_y - y) % 4], 0, keepdims=False)
            term = move(block, to_owner(ka, kb)).astype(F32)
            total = term if total is None else total + term
        sums.append(total)
    flip = (x >> 1) == 1
    grad_weight = jnp.concatenate(
        [jnp.where(flip, sums[1], sums[0]), jnp.where(flip, sums[0], sums[1])], axis=1
    )
    new_weight, new_weight_moment, new_weight_second = adamw_update(
        weight_master, weight_moment, weight_second, grad_weight, step_count
    )
    weight_next = lax.all_gather(new_weight.astype(BF16), "fsdp", axis=0, tiled=True)
    return (
        new_weight,
        new_weight_moment,
        new_weight_second,
        weight_next,
        new_adapter,
        new_adapter_moment,
        new_adapter_second,
        adapter_next,
    )


def solution(mesh):
    return jax.shard_map(
        shards,
        mesh=mesh,
        in_specs=(
            P("fsdp", "tp"),
            P("fsdp", "tp"),
            P(),
            P(),
            P("fsdp", "tp"),
            P("fsdp", "tp"),
            P("fsdp", "tp"),
            P(None, None, "tp", None),
            P(None, None, ("tp", "fsdp"), None),
            P(None, None, ("tp", "fsdp"), None),
            P(None, None, ("tp", "fsdp"), None),
        ),
        out_specs=(
            P("fsdp", "tp"),
            P("fsdp", "tp"),
            P("fsdp", "tp"),
            P(None, "tp"),
            P(None, None, ("tp", "fsdp"), None),
            P(None, None, ("tp", "fsdp"), None),
            P(None, None, ("tp", "fsdp"), None),
            P(None, None, "tp", None),
        ),
        check_vma=False,
    )
```

```python
import functools
import math

import jax
import jax.numpy as jnp
from jax import lax
from jax.experimental import pallas as pl
from jax.experimental.pallas import tpu as pltpu
from jax.sharding import PartitionSpec as P

beta_first = 0.9
beta_second = 0.95
adam_eps = 1e-08
learn_rate = 0.1
decay_rate = 0.1

AXES = ("fsdp", "tp")
X, Y, ZL, ZH, CORE, REGION = range(6)
F32 = jnp.float32
BF16 = jnp.bfloat16


def contract_rows(left, right):
    return lax.dot_general(
        left, right, (((0,), (0,)), ((), ())), preferred_element_type=jnp.float32
    )


def device_number(x, y, zl, zh, c):
    return (zl * 8 + x * 2 + c) * 8 + (y * 2 + zh)


def move(array, where):
    pairs = []
    for x in range(4):
        for y in range(4):
            for zl in range(2):
                for zh in range(2):
                    for c in range(2):
                        a, b, d, e, g = where(x, y, zl, zh, c)
                        pairs.append(
                            (device_number(x, y, zl, zh, c), device_number(a % 4, b % 4, d, e, g))
                        )
    return lax.ppermute(array, AXES, pairs)


def along_x(k):
    return lambda x, y, zl, zh, c: (x + k, y, zl, zh, c)


def along_y(k):
    return lambda x, y, zl, zh, c: (x, y + k, zl, zh, c)


def other_core(x, y, zl, zh, c):
    return (x, y, zl, zh, 1 - c)


def other_zl(x, y, zl, zh, c):
    return (x, y, 1 - zl, zh, c)


def other_zh(x, y, zl, zh, c):
    return (x, y, zl, 1 - zh, c)


def to_owner(ka, kb):
    return lambda x, y, zl, zh, c: (2 * ((x & 1) ^ ka) + zh, y, zl ^ kb, x >> 1, c)


def all_x(array):
    groups = [[z * 8 + x * 2 + c for x in range(4)] for z in range(2) for c in range(2)]
    return lax.all_to_all(array, "fsdp", 0, 0, axis_index_groups=groups)


def all_y(array):
    groups = [[y * 2 + z for y in range(4)] for z in range(2)]
    return lax.all_to_all(array, "tp", 0, 0, axis_index_groups=groups)


def partials_kernel(counts, scale, where, *refs):
    acts, cots, (keep, give) = refs[: sum(counts)], refs[-4:-2], refs[-2:]
    zh, c = where[ZH], where[CORE]
    wide = keep.shape[2]
    for side in range(2):
        place = 2 * (side ^ zh)
        first = 0
        for d, count in enumerate(counts):
            total, row = None, 0
            for ref in acts[first : first + count]:
                term = contract_rows(ref[...], cots[side][pl.ds(row, ref.shape[0]), :])
                total = term if total is None else total + term
                row += ref.shape[0]
            first += count
            total = total * scale
            rows = pl.ds(d * wide, wide)
            for h in range(2):
                part = total[h * wide : (h + 1) * wide]

                @pl.when(c == h)
                def _():
                    keep[place, rows, :] = part[:, :wide].astype(BF16)
                    keep[place + 1, rows, :] = part[:, wide:].astype(BF16)

                @pl.when(c != h)
                def _():
                    give[place, rows, :] = part[:, :wide].astype(BF16)
                    give[place + 1, rows, :] = part[:, wide:].astype(BF16)


def partials(here, acts, cots, scale):
    counts = [len(parts) for parts in acts]
    flat = [part for parts in acts for part in parts]
    wide = flat[0].shape[1] // 2
    shape = (4, len(counts) * wide, wide)
    return pl.pallas_call(
        functools.partial(partials_kernel, counts, scale),
        out_shape=(jax.ShapeDtypeStruct(shape, BF16),) * 2,
        in_specs=[pl.BlockSpec(memory_space=pltpu.SMEM)]
        + [pl.BlockSpec(memory_space=pltpu.VMEM)] * (len(flat) + 2),
        out_specs=(pl.BlockSpec(memory_space=pltpu.VMEM), pl.BlockSpec(memory_space=pltpu.VMEM)),
        compiler_params=pltpu.CompilerParams(vmem_limit_bytes=48 * 1024 * 1024),
    )(here, *flat, *cots)


def low_kernel(scales, where, act, cot, adapters, keep, give):
    rows, rank = keep.shape[0], adapters.shape[3]
    for h in range(2):
        part = pl.ds(h * rows, rows)
        down = jnp.dot(act[part, :], adapters[0, 0], preferred_element_type=F32) * scales[0]
        up = jnp.dot(cot[part, :], adapters[1, 0], preferred_element_type=F32) * scales[1]

        @pl.when(where[ZH] == h)
        def _():
            keep[:, :rank] = down
            keep[:, rank:] = up

        @pl.when(where[ZH] != h)
        def _():
            give[:, :rank] = down.astype(BF16)
            give[:, rank:] = up.astype(BF16)


def low_parts(here, act, cot, adapters, scales):
    rows, rank = act.shape[0] // 2, adapters.shape[3]
    whole = pl.BlockSpec(act.shape, lambda i, where: (0, 0))
    out = pl.BlockSpec((rows, 2 * rank), lambda i, where: (0, 0))
    return pl.pallas_call(
        functools.partial(low_kernel, scales),
        out_shape=(
            jax.ShapeDtypeStruct((rows, 2 * rank), F32),
            jax.ShapeDtypeStruct((rows, 2 * rank), BF16),
        ),
        grid_spec=pltpu.PrefetchScalarGridSpec(
            num_scalar_prefetch=1,
            grid=(1,),
            in_specs=[
                whole,
                whole,
                pl.BlockSpec(
                    (2, 1) + adapters.shape[2:], lambda i, where: (0, where[REGION], 0, 0)
                ),
            ],
            out_specs=(out, out),
        ),
        compiler_params=pltpu.CompilerParams(vmem_limit_bytes=32 * 1024 * 1024),
    )(here, act, cot, adapters)


def grads_kernel(scales, where, low_half, low_other, act, cot, out):
    rows, rank = low_half.shape[0], out.shape[3]
    zh = where[ZH]
    mine = pl.ds(pl.multiple_of(zh * rows, rows), rows)
    theirs = pl.ds(pl.multiple_of((1 - zh) * rows, rows), rows)
    for side, source, start in ((0, act, rank), (1, cot, 0)):
        columns = pl.ds(start, rank)
        total = contract_rows(source[mine, :], low_half[:, columns])
        total = total + contract_rows(source[theirs, :], low_other[:, columns])
        total = (total * scales[side]).astype(BF16)
        for f in range(out.shape[0]):
            out[f, side] = total[f * out.shape[2] : (f + 1) * out.shape[2]]


def adapter_grads(here, low_half, low_other, act, cot, scales, count):
    rank = low_half.shape[1] // 2
    vmem = pl.BlockSpec(memory_space=pltpu.VMEM)
    return pl.pallas_call(
        functools.partial(grads_kernel, scales),
        out_shape=jax.ShapeDtypeStruct((count, 2, act.shape[1] // count, rank), BF16),
        in_specs=[pl.BlockSpec(memory_space=pltpu.SMEM)] + [vmem] * 4,
        out_specs=vmem,
        compiler_params=pltpu.CompilerParams(vmem_limit_bytes=32 * 1024 * 1024),
    )(here, low_half, low_other, act, cot)


def adamw_values(param, moment, second, grad, first_fix, second_fix):
    moment_new = beta_first * moment + (1.0 - beta_first) * grad
    second_new = beta_second * second + (1.0 - beta_second) * grad * grad
    ratio = moment_new / first_fix / (jnp.sqrt(second_new / second_fix) + adam_eps)
    return param - learn_rate * (ratio + decay_rate * param), moment_new, second_new


def adapter_kernel(regions, fixes, got, param, moment, second, *outs):
    new_param, new_moment, new_second, rounded = outs
    rows, rank = param.shape[2:]
    for side in range(2):
        totals = [jnp.zeros((rows, rank), F32) for _ in range(param.shape[1])]
        for f in range(got.shape[0]):
            term = got[f, side].astype(F32)
            totals = [
                total + jnp.where(regions[f] == r, 1.0, 0.0) * term
                for r, total in enumerate(totals)
            ]
        for r, total in enumerate(totals):
            p, m, v = adamw_values(
                param[side, r], moment[side, r], second[side, r], total, fixes[0], fixes[1]
            )
            new_param[side, r] = p
            new_moment[side, r] = m
            new_second[side, r] = v
            rounded[pl.ds((side * param.shape[1] + r) * rows, rows), :] = p.astype(BF16)


def adapter_update(regions, fixes, got, param, moment, second):
    vmem = pl.BlockSpec(memory_space=pltpu.VMEM)
    smem = pl.BlockSpec(memory_space=pltpu.SMEM)
    like = jax.ShapeDtypeStruct(param.shape, F32)
    rounded = jax.ShapeDtypeStruct((math.prod(param.shape[:3]), param.shape[3]), BF16)
    return pl.pallas_call(
        adapter_kernel,
        out_shape=(like, like, like, rounded),
        in_specs=[smem, smem] + [vmem] * 4,
        out_specs=(vmem,) * 4,
        compiler_params=pltpu.CompilerParams(vmem_limit_bytes=32 * 1024 * 1024),
    )(regions, fixes, got, param, moment, second)


def pick_kernel(where, near, far, *outs):
    wide = far.shape[1]
    for k, out in enumerate(outs):
        row_y = 2 * (where[ZL] ^ (k % 2)) + ((where[X] & 1) ^ (k // 2))
        away = (row_y - where[Y] + 4) & 3
        place = away ^ (away >> 1)

        @pl.when(place < 3)
        def _():
            rows = pl.ds(pl.multiple_of(jnp.minimum(place, 2) * wide, wide), wide)
            total = near[0, rows, :].astype(F32)
            for q in range(1, 4):
                total = total + near[q, rows, :].astype(F32)
            out[...] = total.astype(BF16)

        @pl.when(place == 3)
        def _():
            total = far[0].astype(F32)
            for q in range(1, 4):
                total = total + far[q].astype(F32)
            out[...] = total.astype(BF16)


def pick_blocks(here, near, far):
    vmem = pl.BlockSpec(memory_space=pltpu.VMEM)
    count = 4
    return pl.pallas_call(
        pick_kernel,
        out_shape=(jax.ShapeDtypeStruct(far.shape[1:], BF16),) * count,
        in_specs=[pl.BlockSpec(memory_space=pltpu.SMEM), vmem, vmem],
        out_specs=(vmem,) * count,
        compiler_params=pltpu.CompilerParams(vmem_limit_bytes=32 * 1024 * 1024),
    )(here, near, far)


def weight_kernel(where, fixes, *refs):
    terms, (param, moment, second, extra), outs = refs[:4], refs[4:8], refs[8:]
    new_param, new_moment, new_second, rounded = outs
    rows, wide = terms[0].shape
    for ka in range(2):
        grad = terms[2 * ka][...].astype(F32) + terms[2 * ka + 1][...].astype(F32)
        for h in range(2):

            @pl.when(((where[X] >> 1) ^ ka) == h)
            def _():
                columns = pl.ds(h * wide, wide)
                p, m, v = adamw_values(
                    param[:, columns], moment[:, columns], second[:, columns], grad,
                    fixes[0], fixes[1],
                )
                new_param[:, columns] = p
                new_moment[:, columns] = m
                new_second[:, columns] = v
                rounded[pl.ds(h * rows, rows), :] = p.astype(BF16)

    rounded[pl.ds(2 * rows, extra.shape[0]), :] = extra[...]


def weight_update(here, fixes, terms, param, moment, second, extra):
    vmem = pl.BlockSpec(memory_space=pltpu.VMEM)
    smem = pl.BlockSpec(memory_space=pltpu.SMEM)
    like = jax.ShapeDtypeStruct(param.shape, F32)
    rounded = jax.ShapeDtypeStruct((2 * param.shape[0] + extra.shape[0], extra.shape[1]), BF16)
    return pl.pallas_call(
        weight_kernel,
        out_shape=(like, like, like, rounded),
        in_specs=[smem, smem] + [vmem] * 8,
        out_specs=(vmem,) * 4,
        compiler_params=pltpu.CompilerParams(vmem_limit_bytes=32 * 1024 * 1024),
    )(here, fixes, *terms, param, moment, second, extra)


def place_kernel(where, first, second, first_peer, second_peer, weight, adapter):
    chip, c = pl.program_id(0), where[CORE]
    dx, dz = (chip - where[X]) & 3, (chip >> 2) ^ where[ZL]
    near_slot = jnp.where(dx == 0, dz, jnp.where(dx == 3, 2, 3))
    far_slot = jnp.where(dx == 3, 5, jnp.where(dx == 1, 6, 7))
    slot = jnp.where(
        dz == 0, jnp.where(dx == 2, 4, near_slot), jnp.where(dx == 0, dz, far_slot)
    )
    rows, wide = weight.shape[1], weight.shape[2] // 2

    def put(core, block):
        weight[core, :, :wide] = block[:rows]
        weight[core, :, wide:] = block[rows : 2 * rows]
        adapter[:, core] = block[2 * rows :].reshape(adapter.shape[0:1] + adapter.shape[2:])

    for here, low, high in ((c, first, second), (1 - c, first_peer, second_peer)):

        @pl.when(slot < 4)
        def _():
            put(here, low[jnp.minimum(slot, 3)])

        @pl.when(slot >= 4)
        def _():
            put(here, high[jnp.maximum(slot - 4, 0)])


def place_blocks(here, arrays, rows, groups):
    wide = arrays[0].shape[2]
    deep = (arrays[0].shape[1] - 2 * rows) // groups
    return pl.pallas_call(
        place_kernel,
        out_shape=(
            jax.ShapeDtypeStruct((16, rows, 2 * wide), BF16),
            jax.ShapeDtypeStruct((groups, 16, deep, wide), BF16),
        ),
        grid_spec=pltpu.PrefetchScalarGridSpec(
            num_scalar_prefetch=1,
            grid=(8,),
            in_specs=[pl.BlockSpec(array.shape, lambda i, where: (0, 0, 0)) for array in arrays],
            out_specs=(
                pl.BlockSpec((2, rows, 2 * wide), lambda i, where: (i, 0, 0)),
                pl.BlockSpec((groups, 2, deep, wide), lambda i, where: (0, i, 0, 0)),
            ),
        ),
        compiler_params=pltpu.CompilerParams(vmem_limit_bytes=40 * 1024 * 1024),
    )(here, *arrays)


def shards(
    activations,
    cotangent,
    step_count,
    region_of,
    weight_master,
    weight_moment,
    weight_second,
    adapter_copy,
    adapter_master,
    adapter_moment,
    adapter_second,
):
    fsdp_count = lax.axis_size("fsdp")
    tp_count = lax.axis_size("tp")
    tok_dev = activations.shape[0]
    width = activations.shape[1] * tp_count
    rank = adapter_copy.shape[3]
    region_count = adapter_copy.shape[1]
    grad_scale = math.sqrt(width / (tok_dev * fsdp_count))
    inv_width = 1.0 / math.sqrt(width)
    inv_rank = 1.0 / math.sqrt(rank)
    f = lax.axis_index("fsdp")
    t = lax.axis_index("tp")
    zl, x, c = f // 8, (f // 2) % 4, f % 2
    y, zh = t // 2, t % 2

    own_region = lax.dynamic_index_in_dim(region_of, f, 0, keepdims=False)
    here = jnp.stack([x, y, zl, zh, c, own_region]).astype(jnp.int32)
    step_float = step_count[0].astype(F32)
    fixes = jnp.stack([
        1.0 - jnp.power(F32(beta_first), step_float),
        1.0 - jnp.power(F32(beta_second), step_float),
    ])

    middle = tok_dev // 2
    half = activations.shape[1] // 2
    act_first, act_second = activations[:middle], activations[middle:]
    back_first = move(act_first, along_y(1))
    ahead_first = move(act_first, along_y(-1))
    cot_zh = move(cotangent, other_zh)
    back_second = move(act_second, along_y(1))
    ahead_second = move(act_second, along_y(-1))
    far_first = move(back_first, along_y(1))
    far_second = move(ahead_second, along_y(-1))

    low_keep, low_give = low_parts(
        here, activations, cotangent, adapter_copy, (inv_width, inv_rank)
    )
    low_give, back_first, ahead_first, cot_zh = lax.optimization_barrier(
        (low_give, back_first, ahead_first, cot_zh)
    )
    low_half = (low_keep + move(low_give, other_zh).astype(F32)).astype(BF16)
    low_half = low_half.reshape(4, tok_dev // 8, 2 * rank)
    low_half, back_second, ahead_second = lax.optimization_barrier(
        (low_half, back_second, ahead_second)
    )
    low_own = jnp.sum(all_y(low_half).astype(F32), axis=0).astype(BF16)
    low_half = all_y(jnp.broadcast_to(low_own[None], low_half.shape))
    low_half = low_half.reshape(tok_dev // 2, 2 * rank)
    low_other = move(low_half, other_zh)
    parts = adapter_grads(
        here, low_half, low_other, activations, cotangent,
        (inv_width * grad_scale, inv_rank * grad_scale), fsdp_count,
    )
    got = lax.all_to_all(parts, "fsdp", 0, 0)
    new_adapter, new_adapter_moment, new_adapter_second, adapter_rows = adapter_update(
        region_of, fixes, got, adapter_master, adapter_moment, adapter_second
    )

    scale = inv_width * grad_scale
    cots = [cotangent, cot_zh]
    near_keep, near_give = partials(
        here, [[activations], [ahead_first, ahead_second], [back_first, back_second]], cots, scale
    )
    far_first, far_second, near_give = lax.optimization_barrier(
        (far_first, far_second, near_give)
    )
    far_keep, far_give = partials(here, [[far_first, far_second]], cots, scale)

    def reduce_x(keep, give):
        both = (keep.astype(F32) + move(give, other_core).astype(F32)).astype(BF16)
        return all_x(both)

    near = reduce_x(near_keep, near_give)
    far = reduce_x(far_keep, far_give)
    blocks = pick_blocks(here, near, far)
    terms = [move(block, to_owner(k // 2, k % 2)) for k, block in enumerate(blocks)]
    new_weight, new_weight_moment, new_weight_second, piece = weight_update(
        here, fixes, terms, weight_master, weight_moment, weight_second, adapter_rows
    )

    from_zl = move(piece, other_zl)
    from_back = move(piece, along_x(1))
    from_ahead = move(piece, along_x(-1))
    from_far = move(piece, along_x(2))
    first = jnp.stack([piece, from_zl, from_back, from_ahead])
    second = jnp.stack([
        from_far,
        move(from_zl, along_x(1)),
        move(from_zl, along_x(-1)),
        move(from_far, other_zl),
    ])

    weight_next, adapter_next = place_blocks(
        here,
        [first, second, move(first, other_core), move(second, other_core)],
        new_weight.shape[0],
        2 * region_count,
    )
    weight_next = weight_next.reshape(width, -1)
    adapter_next = adapter_next.reshape(adapter_copy.shape)
    return (
        new_weight,
        new_weight_moment,
        new_weight_second,
        weight_next,
        new_adapter,
        new_adapter_moment,
        new_adapter_second,
        adapter_next,
    )


def solution(mesh):
    return jax.shard_map(
        shards,
        mesh=mesh,
        in_specs=(
            P("fsdp", "tp"),
            P("fsdp", "tp"),
            P(),
            P(),
            P("fsdp", "tp"),
            P("fsdp", "tp"),
            P("fsdp", "tp"),
            P(None, None, "tp", None),
            P(None, None, ("tp", "fsdp"), None),
            P(None, None, ("tp", "fsdp"), None),
            P(None, None, ("tp", "fsdp"), None),
        ),
        out_specs=(
            P("fsdp", "tp"),
            P("fsdp", "tp"),
            P("fsdp", "tp"),
            P(None, "tp"),
            P(None, None, ("tp", "fsdp"), None),
            P(None, None, ("tp", "fsdp"), None),
            P(None, None, ("tp", "fsdp"), None),
            P(None, None, "tp", None),
        ),
        check_vma=False,
    )
```

```python
import functools
import math

import jax
import jax.numpy as jnp
from jax import lax
from jax.experimental import pallas as pl
from jax.experimental.pallas import tpu as pltpu
from jax.sharding import PartitionSpec as P

beta_first = 0.9
beta_second = 0.95
adam_eps = 1e-08
learn_rate = 0.1
decay_rate = 0.1

AXES = ("fsdp", "tp")
X, Y, ZL, ZH, CORE, REGION = range(6)
F32 = jnp.float32
BF16 = jnp.bfloat16


def contract_rows(left, right):
    return lax.dot_general(
        left, right, (((0,), (0,)), ((), ())), preferred_element_type=jnp.float32
    )


def device_number(x, y, zl, zh, c):
    return (zl * 8 + x * 2 + c) * 8 + (y * 2 + zh)


def move(array, where):
    pairs = []
    for x in range(4):
        for y in range(4):
            for zl in range(2):
                for zh in range(2):
                    for c in range(2):
                        a, b, d, e, g = where(x, y, zl, zh, c)
                        pairs.append(
                            (device_number(x, y, zl, zh, c), device_number(a % 4, b % 4, d, e, g))
                        )
    return lax.ppermute(array, AXES, pairs)


def swap_among(array, axis, groups):
    return lax.all_to_all(array, axis, 0, 0, axis_index_groups=groups)


X_GROUPS = [[z * 8 + x * 2 + c for x in range(4)] for z in range(2) for c in range(2)]
ZL_X_GROUPS = [[z * 8 + x * 2 + c for z in range(2) for x in range(4)] for c in range(2)]
Y_GROUPS = [[y * 2 + z for y in range(4)] for z in range(2)]


def along_x(k):
    return lambda x, y, zl, zh, c: (x + k, y, zl, zh, c)


def along_y(k):
    return lambda x, y, zl, zh, c: (x, y + k, zl, zh, c)


def other_core(x, y, zl, zh, c):
    return (x, y, zl, zh, 1 - c)


def other_zl(x, y, zl, zh, c):
    return (x, y, 1 - zl, zh, c)


def other_zh(x, y, zl, zh, c):
    return (x, y, zl, 1 - zh, c)


def to_owner(ka, kb):
    return lambda x, y, zl, zh, c: (2 * ((x & 1) ^ ka) + zh, y, zl ^ kb, x >> 1, c)


def partials_kernel(counts, where, *refs):
    acts, (cot, keep, give) = refs[: sum(counts)], refs[-3:]
    c, wide = where[CORE], keep.shape[2]
    for out, h in ((keep, c), (give, 1 - c)):
        half = pl.ds(pl.multiple_of(h * wide, wide), wide)
        first = 0
        for d, count in enumerate(counts):
            for j in range(2):
                total, row = None, 0
                for ref in acts[first : first + count]:
                    block = cot[pl.ds(row, ref.shape[0]), pl.ds(j * wide, wide)]
                    term = contract_rows(ref[:, half], block)
                    total = term if total is None else total + term
                    row += ref.shape[0]
                out[j, pl.ds(d * wide, wide), :] = total.astype(BF16)
            first += count


def partials(here, acts, cot):
    counts = [len(parts) for parts in acts]
    flat = [part for parts in acts for part in parts]
    wide = flat[0].shape[1] // 2
    shape = (2, len(counts) * wide, wide)
    return pl.pallas_call(
        functools.partial(partials_kernel, counts),
        out_shape=(jax.ShapeDtypeStruct(shape, BF16),) * 2,
        in_specs=[pl.BlockSpec(memory_space=pltpu.SMEM)]
        + [pl.BlockSpec(memory_space=pltpu.VMEM)] * (len(flat) + 1),
        out_specs=(pl.BlockSpec(memory_space=pltpu.VMEM), pl.BlockSpec(memory_space=pltpu.VMEM)),
        compiler_params=pltpu.CompilerParams(vmem_limit_bytes=48 * 1024 * 1024),
    )(here, *flat, cot)


def add_kernel(where, *refs):
    parts, outs = refs[:8], refs[8:]
    rows = parts[0].shape[1]
    for k, out in enumerate(outs):
        quarter = (where[X] + k) & 3
        side, j = (quarter >> 1) ^ where[ZH], quarter & 1
        for number in range(2):

            @pl.when(side == number)
            def _():
                keep, got, keep_far, got_far = parts[4 * number : 4 * number + 4]
                out[:rows] = (keep[j].astype(F32) + got[j].astype(F32)).astype(BF16)
                out[rows:] = (keep_far[j].astype(F32) + got_far[j].astype(F32)).astype(BF16)


def add_blocks(here, parts):
    vmem = pl.BlockSpec(memory_space=pltpu.VMEM)
    _, rows, wide = parts[0].shape
    return pl.pallas_call(
        add_kernel,
        out_shape=(jax.ShapeDtypeStruct((rows + parts[2].shape[1], wide), BF16),) * 4,
        in_specs=[pl.BlockSpec(memory_space=pltpu.SMEM)] + [vmem] * 8,
        out_specs=(vmem,) * 4,
        compiler_params=pltpu.CompilerParams(vmem_limit_bytes=32 * 1024 * 1024),
    )(here, *parts)


def low_kernel(scales, where, act, cot, adapters, out):
    rank = adapters.shape[3]
    down = jnp.dot(act[...], adapters[0, 0], preferred_element_type=F32) * scales[0]
    up = jnp.dot(cot[...], adapters[1, 0], preferred_element_type=F32) * scales[1]
    out[:, :rank] = down.astype(BF16)
    out[:, rank:] = up.astype(BF16)


def low_parts(here, act, cot, adapters, scales):
    rank = adapters.shape[3]
    whole = pl.BlockSpec(act.shape, lambda i, where: (0, 0))
    return pl.pallas_call(
        functools.partial(low_kernel, scales),
        out_shape=jax.ShapeDtypeStruct((act.shape[0], 2 * rank), BF16),
        grid_spec=pltpu.PrefetchScalarGridSpec(
            num_scalar_prefetch=1,
            grid=(1,),
            in_specs=[
                whole,
                whole,
                pl.BlockSpec(
                    (2, 1) + adapters.shape[2:], lambda i, where: (0, where[REGION], 0, 0)
                ),
            ],
            out_specs=pl.BlockSpec((act.shape[0], 2 * rank), lambda i, where: (0, 0)),
        ),
        compiler_params=pltpu.CompilerParams(vmem_limit_bytes=32 * 1024 * 1024),
    )(here, act, cot, adapters)


def grads_kernel(scales, low, act, cot, out):
    rank = out.shape[3]
    for side, source, start in ((0, act, rank), (1, cot, 0)):
        total = contract_rows(source[...], low[:, pl.ds(start, rank)])
        total = (total * scales[side]).astype(BF16)
        for f in range(out.shape[0]):
            out[f, side] = total[f * out.shape[2] : (f + 1) * out.shape[2]]


def adapter_grads(low, act, cot, scales, count):
    rank = low.shape[1] // 2
    vmem = pl.BlockSpec(memory_space=pltpu.VMEM)
    return pl.pallas_call(
        functools.partial(grads_kernel, scales),
        out_shape=jax.ShapeDtypeStruct((count, 2, act.shape[1] // count, rank), BF16),
        in_specs=[vmem] * 3,
        out_specs=vmem,
        compiler_params=pltpu.CompilerParams(vmem_limit_bytes=32 * 1024 * 1024),
    )(low, act, cot)


def adamw_values(param, moment, second, grad, first_fix, second_fix):
    moment_new = beta_first * moment + (1.0 - beta_first) * grad
    second_new = beta_second * second + (1.0 - beta_second) * grad * grad
    ratio = moment_new / first_fix / (jnp.sqrt(second_new / second_fix) + adam_eps)
    return param - learn_rate * (ratio + decay_rate * param), moment_new, second_new


def adapter_kernel(regions, fixes, got, param, moment, second, *outs):
    new_param, new_moment, new_second, rounded = outs
    rows, rank = param.shape[2:]
    for side in range(2):
        totals = [jnp.zeros((rows, rank), F32) for _ in range(param.shape[1])]
        for f in range(got.shape[0]):
            term = got[f, side].astype(F32)
            totals = [
                total + jnp.where(regions[f] == r, 1.0, 0.0) * term
                for r, total in enumerate(totals)
            ]
        for r, total in enumerate(totals):
            p, m, v = adamw_values(
                param[side, r], moment[side, r], second[side, r], total, fixes[0], fixes[1]
            )
            new_param[side, r] = p
            new_moment[side, r] = m
            new_second[side, r] = v
            rounded[pl.ds((side * param.shape[1] + r) * rows, rows), :] = p.astype(BF16)


def adapter_update(regions, fixes, got, param, moment, second):
    vmem = pl.BlockSpec(memory_space=pltpu.VMEM)
    smem = pl.BlockSpec(memory_space=pltpu.SMEM)
    like = jax.ShapeDtypeStruct(param.shape, F32)
    rounded = jax.ShapeDtypeStruct((math.prod(param.shape[:3]), param.shape[3]), BF16)
    return pl.pallas_call(
        adapter_kernel,
        out_shape=(like, like, like, rounded),
        in_specs=[smem, smem] + [vmem] * 4,
        out_specs=(vmem,) * 4,
        compiler_params=pltpu.CompilerParams(vmem_limit_bytes=32 * 1024 * 1024),
    )(regions, fixes, got, param, moment, second)


def pick_kernel(where, *refs):
    arrays, outs = refs[:4], refs[4:]
    wide = outs[0].shape[0]
    for k, out in enumerate(outs):
        row_y = 2 * (where[ZL] ^ (k % 2)) + ((where[X] & 1) ^ (k // 2))
        away = (row_y - where[Y] + 4) & 3
        place = away ^ (away >> 1)
        rows = pl.ds(pl.multiple_of(place * wide, wide), wide)
        total = arrays[0][rows, :].astype(F32)
        for array in arrays[1:]:
            total = total + array[rows, :].astype(F32)
        out[...] = total.astype(BF16)


def pick_blocks(here, arrays):
    vmem = pl.BlockSpec(memory_space=pltpu.VMEM)
    rows, columns = arrays[0].shape
    return pl.pallas_call(
        pick_kernel,
        out_shape=(jax.ShapeDtypeStruct((rows // 4, columns), BF16),) * 4,
        in_specs=[pl.BlockSpec(memory_space=pltpu.SMEM)] + [vmem] * 4,
        out_specs=(vmem,) * 4,
        compiler_params=pltpu.CompilerParams(vmem_limit_bytes=32 * 1024 * 1024),
    )(here, *arrays)


def weight_kernel(scale, where, fixes, *refs):
    terms, (param, moment, second, extra), outs = refs[:4], refs[4:8], refs[8:]
    new_param, new_moment, new_second, rounded = outs
    rows, wide = terms[0].shape
    for ka in range(2):
        grad = terms[2 * ka][...].astype(F32) + terms[2 * ka + 1][...].astype(F32)
        grad = grad * scale
        for h in range(2):

            @pl.when(((where[X] >> 1) ^ ka) == h)
            def _():
                columns = pl.ds(h * wide, wide)
                p, m, v = adamw_values(
                    param[:, columns], moment[:, columns], second[:, columns], grad,
                    fixes[0], fixes[1],
                )
                new_param[:, columns] = p
                new_moment[:, columns] = m
                new_second[:, columns] = v
                rounded[pl.ds(h * rows, rows), :] = p.astype(BF16)

    rounded[pl.ds(2 * rows, extra.shape[0]), :] = extra[...]


def weight_update(here, scale, fixes, terms, param, moment, second, extra):
    vmem = pl.BlockSpec(memory_space=pltpu.VMEM)
    smem = pl.BlockSpec(memory_space=pltpu.SMEM)
    like = jax.ShapeDtypeStruct(param.shape, F32)
    rounded = jax.ShapeDtypeStruct((2 * param.shape[0] + extra.shape[0], extra.shape[1]), BF16)
    return pl.pallas_call(
        functools.partial(weight_kernel, scale),
        out_shape=(like, like, like, rounded),
        in_specs=[smem, smem] + [vmem] * 8,
        out_specs=(vmem,) * 4,
        compiler_params=pltpu.CompilerParams(vmem_limit_bytes=32 * 1024 * 1024),
    )(here, fixes, *terms, param, moment, second, extra)


def place_kernel(where, first, second, first_peer, second_peer, weight, adapter):
    chip, c = pl.program_id(0), where[CORE]
    dx, dz = (chip - where[X]) & 3, (chip >> 2) ^ where[ZL]
    near_slot = jnp.where(dx == 0, dz, jnp.where(dx == 3, 2, 3))
    far_slot = jnp.where(dx == 3, 5, jnp.where(dx == 1, 6, 7))
    slot = jnp.where(
        dz == 0, jnp.where(dx == 2, 4, near_slot), jnp.where(dx == 0, dz, far_slot)
    )
    rows, wide = weight.shape[1], weight.shape[2] // 2

    def put(core, block):
        weight[core, :, :wide] = block[:rows]
        weight[core, :, wide:] = block[rows : 2 * rows]
        adapter[:, core] = block[2 * rows :].reshape(adapter.shape[0:1] + adapter.shape[2:])

    for here, low, high in ((c, first, second), (1 - c, first_peer, second_peer)):

        @pl.when(slot < 4)
        def _():
            put(here, low[jnp.minimum(slot, 3)])

        @pl.when(slot >= 4)
        def _():
            put(here, high[jnp.maximum(slot - 4, 0)])


def place_blocks(here, arrays, rows, groups):
    wide = arrays[0].shape[2]
    deep = (arrays[0].shape[1] - 2 * rows) // groups
    return pl.pallas_call(
        place_kernel,
        out_shape=(
            jax.ShapeDtypeStruct((16, rows, 2 * wide), BF16),
            jax.ShapeDtypeStruct((groups, 16, deep, wide), BF16),
        ),
        grid_spec=pltpu.PrefetchScalarGridSpec(
            num_scalar_prefetch=1,
            grid=(8,),
            in_specs=[pl.BlockSpec(array.shape, lambda i, where: (0, 0, 0)) for array in arrays],
            out_specs=(
                pl.BlockSpec((2, rows, 2 * wide), lambda i, where: (i, 0, 0)),
                pl.BlockSpec((groups, 2, deep, wide), lambda i, where: (0, i, 0, 0)),
            ),
        ),
        compiler_params=pltpu.CompilerParams(vmem_limit_bytes=40 * 1024 * 1024),
    )(here, *arrays)


def shards(
    activations,
    cotangent,
    step_count,
    region_of,
    weight_master,
    weight_moment,
    weight_second,
    adapter_copy,
    adapter_master,
    adapter_moment,
    adapter_second,
):
    fsdp_count = lax.axis_size("fsdp")
    tp_count = lax.axis_size("tp")
    tok_dev = activations.shape[0]
    width = activations.shape[1] * tp_count
    rank = adapter_copy.shape[3]
    region_count = adapter_copy.shape[1]
    grad_scale = math.sqrt(width / (tok_dev * fsdp_count))
    inv_width = 1.0 / math.sqrt(width)
    inv_rank = 1.0 / math.sqrt(rank)
    f = lax.axis_index("fsdp")
    t = lax.axis_index("tp")
    zl, x, c = f // 8, (f // 2) % 4, f % 2
    y, zh = t // 2, t % 2

    own_region = lax.dynamic_index_in_dim(region_of, f, 0, keepdims=False)
    here = jnp.stack([x, y, zl, zh, c, own_region]).astype(jnp.int32)
    step_float = step_count[0].astype(F32)
    fixes = jnp.stack([
        1.0 - jnp.power(F32(beta_first), step_float),
        1.0 - jnp.power(F32(beta_second), step_float),
    ])

    middle = tok_dev // 2
    back = move(activations, along_y(1))
    ahead = move(activations, along_y(-1))
    cot_zh = move(cotangent, other_zh)
    far_first = move(back[:middle], along_y(1))
    far_second = move(ahead[middle:], along_y(-1))

    low = low_parts(here, activations, cotangent, adapter_copy, (inv_width, inv_rank))
    low = swap_among(low.reshape(tp_count, tok_dev // tp_count, 2 * rank), "tp", None)
    low_sum = jnp.sum(low.astype(F32), axis=0).astype(BF16)

    def swapped(acts, cot):
        keep, give = partials(here, acts, cot)
        return [keep, move(give, other_core)]

    low_sum, back, ahead = lax.optimization_barrier((low_sum, back, ahead))
    near_acts = [[activations], [ahead], [back]]
    parts = swapped(near_acts, cotangent)
    far_acts = [[far_first, far_second]]
    far_first, far_second, cot_zh = lax.optimization_barrier((far_first, far_second, cot_zh))
    parts += swapped(far_acts, cotangent)
    parts += swapped(near_acts, cot_zh) + swapped(far_acts, cot_zh)
    blocks = add_blocks(here, parts)
    low_sum, *blocks = lax.optimization_barrier((low_sum, *blocks))
    low_all = swap_among(jnp.broadcast_to(low_sum[None], low.shape), "tp", None)
    blocks = [blocks[0]] + [move(blocks[k], along_x(k)) for k in (1, 3, 2)]
    blocks = pick_blocks(here, blocks)
    low_all = low_all.reshape(tok_dev, 2 * rank)

    parts = adapter_grads(
        low_all, activations, cotangent,
        (inv_width * grad_scale, inv_rank * grad_scale), fsdp_count,
    )
    got = lax.all_to_all(parts, "fsdp", 0, 0)
    new_adapter, new_adapter_moment, new_adapter_second, adapter_rows = adapter_update(
        region_of, fixes, got, adapter_master, adapter_moment, adapter_second
    )
    terms = [move(block, to_owner(k // 2, k % 2)) for k, block in enumerate(blocks)]
    new_weight, new_weight_moment, new_weight_second, piece = weight_update(
        here, inv_width * grad_scale, fixes, terms, weight_master, weight_moment, weight_second, adapter_rows
    )

    from_zl = move(piece, other_zl)
    from_back = move(piece, along_x(1))
    from_ahead = move(piece, along_x(-1))
    from_far = move(piece, along_x(2))
    first = jnp.stack([piece, from_zl, from_back, from_ahead])
    second = jnp.stack([
        from_far,
        move(from_zl, along_x(1)),
        move(from_zl, along_x(-1)),
        move(from_far, other_zl),
    ])

    weight_next, adapter_next = place_blocks(
        here,
        [first, second, move(first, other_core), move(second, other_core)],
        new_weight.shape[0],
        2 * region_count,
    )
    weight_next = weight_next.reshape(width, -1)
    adapter_next = adapter_next.reshape(adapter_copy.shape)
    return (
        new_weight,
        new_weight_moment,
        new_weight_second,
        weight_next,
        new_adapter,
        new_adapter_moment,
        new_adapter_second,
        adapter_next,
    )


def solution(mesh):
    return jax.shard_map(
        shards,
        mesh=mesh,
        in_specs=(
            P("fsdp", "tp"),
            P("fsdp", "tp"),
            P(),
            P(),
            P("fsdp", "tp"),
            P("fsdp", "tp"),
            P("fsdp", "tp"),
            P(None, None, "tp", None),
            P(None, None, ("tp", "fsdp"), None),
            P(None, None, ("tp", "fsdp"), None),
            P(None, None, ("tp", "fsdp"), None),
        ),
        out_specs=(
            P("fsdp", "tp"),
            P("fsdp", "tp"),
            P("fsdp", "tp"),
            P(None, "tp"),
            P(None, None, ("tp", "fsdp"), None),
            P(None, None, ("tp", "fsdp"), None),
            P(None, None, ("tp", "fsdp"), None),
            P(None, None, "tp", None),
        ),
        check_vma=False,
    )
```

```python
import functools
import math

import jax
import jax.numpy as jnp
from jax import lax
from jax.experimental import pallas as pl
from jax.experimental.pallas import tpu as pltpu
from jax.sharding import PartitionSpec as P

beta_first = 0.9
beta_second = 0.95
adam_eps = 1e-08
learn_rate = 0.1
decay_rate = 0.1

AXES = ("fsdp", "tp")
X, Y, ZL, ZH, CORE, REGION = range(6)
F32 = jnp.float32
BF16 = jnp.bfloat16


def contract_rows(left, right):
    return lax.dot_general(
        left, right, (((0,), (0,)), ((), ())), preferred_element_type=jnp.float32
    )


def device_number(x, y, zl, zh, c):
    return (zl * 8 + x * 2 + c) * 8 + (y * 2 + zh)


def move(array, where):
    pairs = []
    for x in range(4):
        for y in range(4):
            for zl in range(2):
                for zh in range(2):
                    for c in range(2):
                        a, b, d, e, g = where(x, y, zl, zh, c)
                        pairs.append(
                            (device_number(x, y, zl, zh, c), device_number(a % 4, b % 4, d, e, g))
                        )
    return lax.ppermute(array, AXES, pairs)


def swap_among(array, axis, groups):
    return lax.all_to_all(array, axis, 0, 0, axis_index_groups=groups)


X_GROUPS = [[z * 8 + x * 2 + c for x in range(4)] for z in range(2) for c in range(2)]
ZL_X_GROUPS = [[z * 8 + x * 2 + c for z in range(2) for x in range(4)] for c in range(2)]
Y_GROUPS = [[y * 2 + z for y in range(4)] for z in range(2)]


def along_x(k):
    return lambda x, y, zl, zh, c: (x + k, y, zl, zh, c)


def along_y(k):
    return lambda x, y, zl, zh, c: (x, y + k, zl, zh, c)


def other_core(x, y, zl, zh, c):
    return (x, y, zl, zh, 1 - c)


def other_zl(x, y, zl, zh, c):
    return (x, y, 1 - zl, zh, c)


def other_zh(x, y, zl, zh, c):
    return (x, y, zl, 1 - zh, c)


def to_owner(ka, kb):
    return lambda x, y, zl, zh, c: (2 * ((x & 1) ^ ka) + zh, y, zl ^ kb, x >> 1, c)


def partials_kernel(counts, where, *refs):
    acts, (cot, keep, give) = refs[: sum(counts)], refs[-3:]
    c, wide = where[CORE], keep.shape[2]
    for out, h in ((keep, c), (give, 1 - c)):
        half = pl.ds(pl.multiple_of(h * wide, wide), wide)
        first = 0
        for d, count in enumerate(counts):
            for j in range(2):
                total, row = None, 0
                for ref in acts[first : first + count]:
                    block = cot[pl.ds(row, ref.shape[0]), pl.ds(j * wide, wide)]
                    term = contract_rows(ref[:, half], block)
                    total = term if total is None else total + term
                    row += ref.shape[0]
                out[j, pl.ds(d * wide, wide), :] = total.astype(BF16)
            first += count


def partials(here, acts, cot):
    counts = [len(parts) for parts in acts]
    flat = [part for parts in acts for part in parts]
    wide = flat[0].shape[1] // 2
    shape = (2, len(counts) * wide, wide)
    return pl.pallas_call(
        functools.partial(partials_kernel, counts),
        out_shape=(jax.ShapeDtypeStruct(shape, BF16),) * 2,
        in_specs=[pl.BlockSpec(memory_space=pltpu.SMEM)]
        + [pl.BlockSpec(memory_space=pltpu.VMEM)] * (len(flat) + 1),
        out_specs=(pl.BlockSpec(memory_space=pltpu.VMEM), pl.BlockSpec(memory_space=pltpu.VMEM)),
        compiler_params=pltpu.CompilerParams(vmem_limit_bytes=48 * 1024 * 1024),
    )(here, *flat, cot)


def add_kernel(where, *refs):
    parts, outs = refs[:8], refs[8:]
    rows = parts[0].shape[1]
    for k, out in enumerate(outs):
        quarter = (where[X] + k) & 3
        side, j = (quarter >> 1) ^ where[ZH], quarter & 1
        for number in range(2):

            @pl.when(side == number)
            def _():
                keep, got, keep_far, got_far = parts[4 * number : 4 * number + 4]
                out[:rows] = (keep[j].astype(F32) + got[j].astype(F32)).astype(BF16)
                out[rows:] = (keep_far[j].astype(F32) + got_far[j].astype(F32)).astype(BF16)


def add_blocks(here, parts):
    vmem = pl.BlockSpec(memory_space=pltpu.VMEM)
    _, rows, wide = parts[0].shape
    return pl.pallas_call(
        add_kernel,
        out_shape=(jax.ShapeDtypeStruct((rows + parts[2].shape[1], wide), BF16),) * 4,
        in_specs=[pl.BlockSpec(memory_space=pltpu.SMEM)] + [vmem] * 8,
        out_specs=(vmem,) * 4,
        compiler_params=pltpu.CompilerParams(vmem_limit_bytes=32 * 1024 * 1024),
    )(here, *parts)


def low_kernel(scales, where, act, cot, adapters, keep, give):
    rows, rank = keep.shape[0], adapters.shape[3]
    for out, h in ((keep, where[ZH]), (give, 1 - where[ZH])):
        part = pl.ds(pl.multiple_of(h * rows, rows), rows)
        down = jnp.dot(act[part, :], adapters[0, 0], preferred_element_type=F32) * scales[0]
        up = jnp.dot(cot[part, :], adapters[1, 0], preferred_element_type=F32) * scales[1]
        out[:, :rank] = down.astype(out.dtype)
        out[:, rank:] = up.astype(out.dtype)


def low_parts(here, act, cot, adapters, scales):
    rows, rank = act.shape[0] // 2, adapters.shape[3]
    whole = pl.BlockSpec(act.shape, lambda i, where: (0, 0))
    out = pl.BlockSpec((rows, 2 * rank), lambda i, where: (0, 0))
    return pl.pallas_call(
        functools.partial(low_kernel, scales),
        out_shape=(
            jax.ShapeDtypeStruct((rows, 2 * rank), F32),
            jax.ShapeDtypeStruct((rows, 2 * rank), BF16),
        ),
        grid_spec=pltpu.PrefetchScalarGridSpec(
            num_scalar_prefetch=1,
            grid=(1,),
            in_specs=[
                whole,
                whole,
                pl.BlockSpec(
                    (2, 1) + adapters.shape[2:], lambda i, where: (0, where[REGION], 0, 0)
                ),
            ],
            out_specs=(out, out),
        ),
        compiler_params=pltpu.CompilerParams(vmem_limit_bytes=32 * 1024 * 1024),
    )(here, act, cot, adapters)


def low_add_kernel(keep, got, out):
    out[...] = (keep[...] + got[...].astype(F32)).astype(BF16)


def low_add(keep, got):
    vmem = pl.BlockSpec(memory_space=pltpu.VMEM)
    return pl.pallas_call(
        low_add_kernel,
        out_shape=jax.ShapeDtypeStruct(keep.shape, BF16),
        in_specs=[vmem, vmem],
        out_specs=vmem,
        compiler_params=pltpu.CompilerParams(vmem_limit_bytes=16 * 1024 * 1024),
    )(keep, got)


def sum_kernel(parts, out):
    total = parts[0].astype(F32)
    for i in range(1, parts.shape[0]):
        total = total + parts[i].astype(F32)
    out[...] = total.astype(BF16)


def sum_parts(parts):
    vmem = pl.BlockSpec(memory_space=pltpu.VMEM)
    return pl.pallas_call(
        sum_kernel,
        out_shape=jax.ShapeDtypeStruct(parts.shape[1:], BF16),
        in_specs=[vmem],
        out_specs=vmem,
        compiler_params=pltpu.CompilerParams(vmem_limit_bytes=16 * 1024 * 1024),
    )(parts)


def grads_kernel(scales, where, *refs):
    pieces, (act, cot, out, low) = refs[:4], refs[4:]
    rows, rank = pieces[0].shape[1], out.shape[3]
    for k, piece in enumerate(pieces):
        for other in range(2):
            place = 4 * (where[ZH] ^ other) + ((where[Y] - k + 4) & 3)
            low[pl.ds(pl.multiple_of(place * rows, rows), rows), :] = piece[other]
    for side, source, start in ((0, act, rank), (1, cot, 0)):
        total = contract_rows(source[...], low[:, pl.ds(start, rank)])
        total = (total * scales[side]).astype(BF16)
        for f in range(out.shape[0]):
            out[f, side] = total[f * out.shape[2] : (f + 1) * out.shape[2]]


def adapter_grads(here, pieces, act, cot, scales, count):
    rank = pieces[0].shape[2] // 2
    vmem = pl.BlockSpec(memory_space=pltpu.VMEM)
    return pl.pallas_call(
        functools.partial(grads_kernel, scales),
        out_shape=jax.ShapeDtypeStruct((count, 2, act.shape[1] // count, rank), BF16),
        in_specs=[pl.BlockSpec(memory_space=pltpu.SMEM)] + [vmem] * 6,
        out_specs=vmem,
        scratch_shapes=[pltpu.VMEM((act.shape[0], 2 * rank), BF16)],
        compiler_params=pltpu.CompilerParams(vmem_limit_bytes=32 * 1024 * 1024),
    )(here, *pieces, act, cot)


def adamw_values(param, moment, second, grad, first_fix, second_fix):
    moment_new = beta_first * moment + (1.0 - beta_first) * grad
    second_new = beta_second * second + (1.0 - beta_second) * grad * grad
    ratio = moment_new / first_fix / (jnp.sqrt(second_new / second_fix) + adam_eps)
    return param - learn_rate * (ratio + decay_rate * param), moment_new, second_new


def adapter_kernel(regions, fixes, got, param, moment, second, *outs):
    new_param, new_moment, new_second, rounded = outs
    rows, rank = param.shape[2:]
    for side in range(2):
        totals = [jnp.zeros((rows, rank), F32) for _ in range(param.shape[1])]
        for f in range(got.shape[0]):
            term = got[f, side].astype(F32)
            totals = [
                total + jnp.where(regions[f] == r, 1.0, 0.0) * term
                for r, total in enumerate(totals)
            ]
        for r, total in enumerate(totals):
            p, m, v = adamw_values(
                param[side, r], moment[side, r], second[side, r], total, fixes[0], fixes[1]
            )
            new_param[side, r] = p
            new_moment[side, r] = m
            new_second[side, r] = v
            rounded[pl.ds((side * param.shape[1] + r) * rows, rows), :] = p.astype(BF16)


def adapter_update(regions, fixes, got, param, moment, second):
    vmem = pl.BlockSpec(memory_space=pltpu.VMEM)
    smem = pl.BlockSpec(memory_space=pltpu.SMEM)
    like = jax.ShapeDtypeStruct(param.shape, F32)
    rounded = jax.ShapeDtypeStruct((math.prod(param.shape[:3]), param.shape[3]), BF16)
    return pl.pallas_call(
        adapter_kernel,
        out_shape=(like, like, like, rounded),
        in_specs=[smem, smem] + [vmem] * 4,
        out_specs=(vmem,) * 4,
        compiler_params=pltpu.CompilerParams(vmem_limit_bytes=32 * 1024 * 1024),
    )(regions, fixes, got, param, moment, second)


def pick_kernel(where, *refs):
    arrays, outs = refs[:4], refs[4:]
    wide = outs[0].shape[0]
    for k, out in enumerate(outs):
        row_y = 2 * (where[ZL] ^ (k % 2)) + ((where[X] & 1) ^ (k // 2))
        away = (row_y - where[Y] + 4) & 3
        place = away ^ (away >> 1)
        rows = pl.ds(pl.multiple_of(place * wide, wide), wide)
        total = arrays[0][rows, :].astype(F32)
        for array in arrays[1:]:
            total = total + array[rows, :].astype(F32)
        out[...] = total.astype(BF16)


def pick_blocks(here, arrays):
    vmem = pl.BlockSpec(memory_space=pltpu.VMEM)
    rows, columns = arrays[0].shape
    return pl.pallas_call(
        pick_kernel,
        out_shape=(jax.ShapeDtypeStruct((rows // 4, columns), BF16),) * 4,
        in_specs=[pl.BlockSpec(memory_space=pltpu.SMEM)] + [vmem] * 4,
        out_specs=(vmem,) * 4,
        compiler_params=pltpu.CompilerParams(vmem_limit_bytes=32 * 1024 * 1024),
    )(here, *arrays)


def weight_kernel(scale, where, fixes, *refs):
    terms, (param, moment, second, extra), outs = refs[:4], refs[4:8], refs[8:]
    new_param, new_moment, new_second, rounded = outs
    rows, wide = terms[0].shape
    for ka in range(2):
        grad = terms[2 * ka][...].astype(F32) + terms[2 * ka + 1][...].astype(F32)
        grad = grad * scale
        for h in range(2):

            @pl.when(((where[X] >> 1) ^ ka) == h)
            def _():
                columns = pl.ds(h * wide, wide)
                p, m, v = adamw_values(
                    param[:, columns], moment[:, columns], second[:, columns], grad,
                    fixes[0], fixes[1],
                )
                new_param[:, columns] = p
                new_moment[:, columns] = m
                new_second[:, columns] = v
                rounded[pl.ds(h * rows, rows), :] = p.astype(BF16)

    rounded[pl.ds(2 * rows, extra.shape[0]), :] = extra[...]


def weight_update(here, scale, fixes, terms, param, moment, second, extra):
    vmem = pl.BlockSpec(memory_space=pltpu.VMEM)
    smem = pl.BlockSpec(memory_space=pltpu.SMEM)
    like = jax.ShapeDtypeStruct(param.shape, F32)
    rounded = jax.ShapeDtypeStruct((2 * param.shape[0] + extra.shape[0], extra.shape[1]), BF16)
    return pl.pallas_call(
        functools.partial(weight_kernel, scale),
        out_shape=(like, like, like, rounded),
        in_specs=[smem, smem] + [vmem] * 8,
        out_specs=(vmem,) * 4,
        compiler_params=pltpu.CompilerParams(vmem_limit_bytes=32 * 1024 * 1024),
    )(here, fixes, *terms, param, moment, second, extra)


def place_kernel(slots, where, own, peer, *refs):
    weight, adapter = refs[-2:]
    rows, wide = weight.shape[1], weight.shape[2] // 2
    for core, source in ((where[CORE], own), (1 - where[CORE], peer)):
        block = source[pl.program_id(0)]
        weight[core, :, :wide] = block[:rows]
        weight[core, :, wide:] = block[rows : 2 * rows]
        adapter[:, core] = block[2 * rows :].reshape(adapter.shape[0:1] + adapter.shape[2:])


def place_blocks(here, slots, own, peer, rows, groups, outs):
    wide = own.shape[2]
    deep = (own.shape[1] - 2 * rows) // groups

    def chip(i, where):
        dx, dz = (functools.reduce(lambda rest, s: jnp.where(i == s[0], s[1], rest), enumerate(axis), 0) for axis in zip(*slots))
        return ((where[ZL] ^ dz) << 2) + ((where[X] + dx) & 3)

    def block(i, where):
        return (0, 0, 0)

    shapes = (
        jax.ShapeDtypeStruct((16, rows, 2 * wide), BF16),
        jax.ShapeDtypeStruct((groups, 16, deep, wide), BF16),
    )
    return pl.pallas_call(
        functools.partial(place_kernel, slots),
        out_shape=shapes,
        grid_spec=pltpu.PrefetchScalarGridSpec(
            num_scalar_prefetch=1,
            grid=(len(slots),),
            in_specs=[pl.BlockSpec(own.shape, block), pl.BlockSpec(own.shape, block)]
            + [pl.BlockSpec(memory_space=pl.ANY)] * len(outs),
            out_specs=(
                pl.BlockSpec((2, rows, 2 * wide), lambda i, where: (chip(i, where), 0, 0)),
                pl.BlockSpec((groups, 2, deep, wide), lambda i, where: (0, chip(i, where), 0, 0)),
            ),
        ),
        input_output_aliases={3: 0, 4: 1} if outs else {},
        compiler_params=pltpu.CompilerParams(vmem_limit_bytes=24 * 1024 * 1024),
    )(here, own, peer, *outs)


def shards(
    activations,
    cotangent,
    step_count,
    region_of,
    weight_master,
    weight_moment,
    weight_second,
    adapter_copy,
    adapter_master,
    adapter_moment,
    adapter_second,
):
    fsdp_count = lax.axis_size("fsdp")
    tp_count = lax.axis_size("tp")
    tok_dev = activations.shape[0]
    width = activations.shape[1] * tp_count
    rank = adapter_copy.shape[3]
    region_count = adapter_copy.shape[1]
    grad_scale = math.sqrt(width / (tok_dev * fsdp_count))
    inv_width = 1.0 / math.sqrt(width)
    inv_rank = 1.0 / math.sqrt(rank)
    f = lax.axis_index("fsdp")
    t = lax.axis_index("tp")
    zl, x, c = f // 8, (f // 2) % 4, f % 2
    y, zh = t // 2, t % 2

    own_region = lax.dynamic_index_in_dim(region_of, f, 0, keepdims=False)
    here = jnp.stack([x, y, zl, zh, c, own_region]).astype(jnp.int32)
    step_float = step_count[0].astype(F32)
    fixes = jnp.stack([
        1.0 - jnp.power(F32(beta_first), step_float),
        1.0 - jnp.power(F32(beta_second), step_float),
    ])

    low_keep, low_give = low_parts(
        here, activations, cotangent, adapter_copy, (inv_width, inv_rank)
    )
    low_got = move(low_give, other_zh)

    middle = tok_dev // 2
    back = move(activations, along_y(1))
    ahead = move(activations, along_y(-1))
    low_got, cot_give, back_half, ahead_half = lax.optimization_barrier(
        (low_got, cotangent, back[:middle], ahead[middle:])
    )
    cot_zh = move(cot_give, other_zh)
    far_first = move(back_half, along_y(1))
    far_second = move(ahead_half, along_y(-1))

    low = low_add(low_keep, low_got).reshape(4, tok_dev // 8, 2 * rank)
    low_sum = sum_parts(swap_among(low, "tp", Y_GROUPS))

    def swapped(acts, cot):
        keep, give = partials(here, acts, cot)
        return [keep, move(give, other_core)]

    low_sum, back, ahead, far_first, far_second = lax.optimization_barrier(
        (low_sum, back, ahead, far_first, far_second)
    )
    low_both = jnp.stack([low_sum, move(low_sum, other_zh)])
    near_acts, far_acts = [[activations], [ahead], [back]], [[far_first, far_second]]
    parts = swapped(near_acts, cotangent) + swapped(far_acts, cotangent)
    parts += swapped(near_acts, cot_zh) + swapped(far_acts, cot_zh)
    blocks = add_blocks(here, parts)
    low_pieces = [low_both] + [move(low_both, along_y(k)) for k in (1, 2, 3)]
    blocks = [blocks[0]] + [move(blocks[k], along_x(k)) for k in (1, 3, 2)]
    blocks = pick_blocks(here, blocks)

    parts = adapter_grads(
        here, low_pieces, activations, cotangent,
        (inv_width * grad_scale, inv_rank * grad_scale), fsdp_count,
    )
    got = lax.all_to_all(parts, "fsdp", 0, 0)
    new_adapter, new_adapter_moment, new_adapter_second, adapter_rows = adapter_update(
        region_of, fixes, got, adapter_master, adapter_moment, adapter_second
    )
    terms = [move(block, to_owner(k // 2, k % 2)) for k, block in enumerate(blocks)]
    new_weight, new_weight_moment, new_weight_second, piece = weight_update(
        here, inv_width * grad_scale, fixes, terms, weight_master, weight_moment, weight_second, adapter_rows
    )

    from_zl = move(piece, other_zl)
    from_back = move(piece, along_x(1))
    from_ahead = move(piece, along_x(-1))
    from_far = move(piece, along_x(2))
    first = jnp.stack([piece, from_zl, from_back, from_ahead])
    second = jnp.stack([
        from_far,
        move(from_zl, along_x(1)),
        move(from_zl, along_x(-1)),
        move(from_far, other_zl),
    ])

    outs = ()
    for slots, blocks in (
        (((0, 0), (0, 1), (-1, 0), (1, 0)), first),
        (((2, 0), (-1, 1), (1, 1), (2, 1)), second),
    ):
        outs = place_blocks(
            here, slots, blocks, move(blocks, other_core), new_weight.shape[0],
            2 * region_count, outs,
        )
    weight_next = outs[0].reshape(width, -1)
    adapter_next = outs[1].reshape(adapter_copy.shape)
    return (
        new_weight,
        new_weight_moment,
        new_weight_second,
        weight_next,
        new_adapter,
        new_adapter_moment,
        new_adapter_second,
        adapter_next,
    )


def solution(mesh):
    return jax.shard_map(
        shards,
        mesh=mesh,
        in_specs=(
            P("fsdp", "tp"),
            P("fsdp", "tp"),
            P(),
            P(),
            P("fsdp", "tp"),
            P("fsdp", "tp"),
            P("fsdp", "tp"),
            P(None, None, "tp", None),
            P(None, None, ("tp", "fsdp"), None),
            P(None, None, ("tp", "fsdp"), None),
            P(None, None, ("tp", "fsdp"), None),
        ),
        out_specs=(
            P("fsdp", "tp"),
            P("fsdp", "tp"),
            P("fsdp", "tp"),
            P(None, "tp"),
            P(None, None, ("tp", "fsdp"), None),
            P(None, None, ("tp", "fsdp"), None),
            P(None, None, ("tp", "fsdp"), None),
            P(None, None, "tp", None),
        ),
        check_vma=False,
    )
```

```python
import functools
import math

import jax
import jax.numpy as jnp
from jax import lax
from jax.experimental import pallas as pl
from jax.experimental.pallas import tpu as pltpu
from jax.sharding import PartitionSpec as P

beta_first = 0.9
beta_second = 0.95
adam_eps = 1e-08
learn_rate = 0.1
decay_rate = 0.1

AXES = ("fsdp", "tp")
X, Y, ZL, ZH, CORE, FSDP = range(6)
F32 = jnp.float32
BF16 = jnp.bfloat16


def contract_rows(left, right):
    return lax.dot_general(
        left, right, (((0,), (0,)), ((), ())), preferred_element_type=jnp.float32
    )


def device_number(x, y, zl, zh, c):
    return (zl * 8 + x * 2 + c) * 8 + (y * 2 + zh)


def move(array, where):
    pairs = []
    for x in range(4):
        for y in range(4):
            for zl in range(2):
                for zh in range(2):
                    for c in range(2):
                        a, b, d, e, g = where(x, y, zl, zh, c)
                        pairs.append(
                            (device_number(x, y, zl, zh, c), device_number(a % 4, b % 4, d, e, g))
                        )
    return lax.ppermute(array, AXES, pairs)


def swap_among(array, axis, groups):
    return lax.all_to_all(array, axis, 0, 0, axis_index_groups=groups)


X_GROUPS = [[z * 8 + x * 2 + c for x in range(4)] for z in range(2) for c in range(2)]
ZL_X_GROUPS = [[z * 8 + x * 2 + c for z in range(2) for x in range(4)] for c in range(2)]
Y_GROUPS = [[y * 2 + z for y in range(4)] for z in range(2)]


def along_x(k):
    return lambda x, y, zl, zh, c: (x + k, y, zl, zh, c)


def along_y(k):
    return lambda x, y, zl, zh, c: (x, y + k, zl, zh, c)


def other_core(x, y, zl, zh, c):
    return (x, y, zl, zh, 1 - c)


def other_zl(x, y, zl, zh, c):
    return (x, y, 1 - zl, zh, c)


def other_zh(x, y, zl, zh, c):
    return (x, y, zl, 1 - zh, c)


def to_owner(ka, kb):
    return lambda x, y, zl, zh, c: (2 * ((x & 1) ^ ka) + zh, y, zl ^ kb, x >> 1, c)


def partials_kernel(counts, where, *refs):
    acts, (cot, keep, give) = refs[: sum(counts)], refs[-3:]
    c, wide = where[CORE], keep.shape[2]
    for out, h in ((keep, c), (give, 1 - c)):
        half = pl.ds(pl.multiple_of(h * wide, wide), wide)
        first = 0
        for d, count in enumerate(counts):
            for j in range(2):
                total, row = None, 0
                for ref in acts[first : first + count]:
                    block = cot[pl.ds(row, ref.shape[0]), pl.ds(j * wide, wide)]
                    term = contract_rows(ref[:, half], block)
                    total = term if total is None else total + term
                    row += ref.shape[0]
                out[j, pl.ds(d * wide, wide), :] = total.astype(BF16)
            first += count


def partials(here, acts, cot):
    counts = [len(parts) for parts in acts]
    flat = [part for parts in acts for part in parts]
    wide = flat[0].shape[1] // 2
    shape = (2, len(counts) * wide, wide)
    return pl.pallas_call(
        functools.partial(partials_kernel, counts),
        out_shape=(jax.ShapeDtypeStruct(shape, BF16),) * 2,
        in_specs=[pl.BlockSpec(memory_space=pltpu.SMEM)]
        + [pl.BlockSpec(memory_space=pltpu.VMEM)] * (len(flat) + 1),
        out_specs=(pl.BlockSpec(memory_space=pltpu.VMEM), pl.BlockSpec(memory_space=pltpu.VMEM)),
        compiler_params=pltpu.CompilerParams(vmem_limit_bytes=48 * 1024 * 1024),
    )(here, *flat, cot)


def add_kernel(where, *refs):
    parts, outs = refs[:8], refs[8:]
    rows = parts[0].shape[1]
    for k, out in enumerate(outs):
        quarter = (where[X] + k) & 3
        side, j = (quarter >> 1) ^ where[ZH], quarter & 1
        for number in range(2):

            @pl.when(side == number)
            def _():
                keep, got, keep_far, got_far = parts[4 * number : 4 * number + 4]
                out[:rows] = (keep[j].astype(F32) + got[j].astype(F32)).astype(BF16)
                out[rows:] = (keep_far[j].astype(F32) + got_far[j].astype(F32)).astype(BF16)


def add_blocks(here, parts):
    vmem = pl.BlockSpec(memory_space=pltpu.VMEM)
    _, rows, wide = parts[0].shape
    return pl.pallas_call(
        add_kernel,
        out_shape=(jax.ShapeDtypeStruct((rows + parts[2].shape[1], wide), BF16),) * 4,
        in_specs=[pl.BlockSpec(memory_space=pltpu.SMEM)] + [vmem] * 8,
        out_specs=(vmem,) * 4,
        compiler_params=pltpu.CompilerParams(vmem_limit_bytes=32 * 1024 * 1024),
    )(here, *parts)


def low_kernel(scales, where, regions, act, cot, adapters, keep, give, acts, cots, own, sems):
    rows, rank = keep.shape[0], own.shape[2]
    region = regions[where[FSDP]]
    copies = [
        pltpu.make_async_copy(adapters.at[0, region], own.at[0], sems.at[0]),
        pltpu.make_async_copy(act, acts, sems.at[1]),
        pltpu.make_async_copy(adapters.at[1, region], own.at[1], sems.at[2]),
        pltpu.make_async_copy(cot, cots, sems.at[3]),
    ]
    for copy in copies:
        copy.start()
    for side, source in enumerate((acts, cots)):
        copies[2 * side].wait()
        copies[2 * side + 1].wait()
        columns = pl.ds(side * rank, rank)
        for out, h in ((keep, where[ZH]), (give, 1 - where[ZH])):
            part = source[pl.ds(pl.multiple_of(h * rows, rows), rows), :]
            total = jnp.dot(part, own[side], preferred_element_type=F32) * scales[side]
            out[:, columns] = total.astype(out.dtype)


def low_parts(here, regions, act, cot, adapters, scales):
    rows, rank = act.shape[0] // 2, adapters.shape[3]
    smem = pl.BlockSpec(memory_space=pltpu.SMEM)
    hbm = pl.BlockSpec(memory_space=pltpu.HBM)
    vmem = pl.BlockSpec(memory_space=pltpu.VMEM)
    return pl.pallas_call(
        functools.partial(low_kernel, scales),
        out_shape=(
            jax.ShapeDtypeStruct((rows, 2 * rank), F32),
            jax.ShapeDtypeStruct((rows, 2 * rank), BF16),
        ),
        in_specs=[smem, smem, hbm, hbm, hbm],
        out_specs=(vmem, vmem),
        scratch_shapes=[
            pltpu.VMEM(act.shape, BF16),
            pltpu.VMEM(cot.shape, BF16),
            pltpu.VMEM((2,) + adapters.shape[2:], BF16),
            pltpu.SemaphoreType.DMA((4,)),
        ],
        compiler_params=pltpu.CompilerParams(vmem_limit_bytes=24 * 1024 * 1024),
    )(here, regions, act, cot, adapters)


def low_add_kernel(keep, got, out):
    out[...] = (keep[...] + got[...].astype(F32)).astype(BF16)


def low_add(keep, got):
    vmem = pl.BlockSpec(memory_space=pltpu.VMEM)
    return pl.pallas_call(
        low_add_kernel,
        out_shape=jax.ShapeDtypeStruct(keep.shape, BF16),
        in_specs=[vmem, vmem],
        out_specs=vmem,
        compiler_params=pltpu.CompilerParams(vmem_limit_bytes=16 * 1024 * 1024),
    )(keep, got)


def sum_kernel(parts, out):
    total = parts[0].astype(F32)
    for i in range(1, parts.shape[0]):
        total = total + parts[i].astype(F32)
    out[...] = total.astype(BF16)


def sum_parts(parts):
    vmem = pl.BlockSpec(memory_space=pltpu.VMEM)
    return pl.pallas_call(
        sum_kernel,
        out_shape=jax.ShapeDtypeStruct(parts.shape[1:], BF16),
        in_specs=[vmem],
        out_specs=vmem,
        compiler_params=pltpu.CompilerParams(vmem_limit_bytes=16 * 1024 * 1024),
    )(parts)


def grads_kernel(scales, where, *refs):
    pieces, (act, cot, out, low) = refs[:4], refs[4:]
    rows, rank = pieces[0].shape[1], out.shape[3]
    for k, piece in enumerate(pieces):
        for other in range(2):
            place = 4 * (where[ZH] ^ other) + ((where[Y] - k + 4) & 3)
            low[pl.ds(pl.multiple_of(place * rows, rows), rows), :] = piece[other]
    for side, source, start in ((0, act, rank), (1, cot, 0)):
        total = contract_rows(source[...], low[:, pl.ds(start, rank)])
        total = (total * scales[side]).astype(BF16)
        for f in range(out.shape[0]):
            out[f, side] = total[f * out.shape[2] : (f + 1) * out.shape[2]]


def adapter_grads(here, pieces, act, cot, scales, count):
    rank = pieces[0].shape[2] // 2
    vmem = pl.BlockSpec(memory_space=pltpu.VMEM)
    return pl.pallas_call(
        functools.partial(grads_kernel, scales),
        out_shape=jax.ShapeDtypeStruct((count, 2, act.shape[1] // count, rank), BF16),
        in_specs=[pl.BlockSpec(memory_space=pltpu.SMEM)] + [vmem] * 6,
        out_specs=vmem,
        scratch_shapes=[pltpu.VMEM((act.shape[0], 2 * rank), BF16)],
        compiler_params=pltpu.CompilerParams(vmem_limit_bytes=32 * 1024 * 1024),
    )(here, *pieces, act, cot)


def adamw_values(param, moment, second, grad, first_fix, second_fix):
    moment_new = beta_first * moment + (1.0 - beta_first) * grad
    second_new = beta_second * second + (1.0 - beta_second) * grad * grad
    ratio = moment_new / first_fix / (jnp.sqrt(second_new / second_fix) + adam_eps)
    return param - learn_rate * (ratio + decay_rate * param), moment_new, second_new


def adapter_kernel(regions, fixes, got, *refs):
    states, (new_param, new_moment, new_second, rounded), held, sums, sems = (
        refs[:3], refs[3:7], refs[7:10], refs[10], refs[11]
    )
    copies = [
        pltpu.make_async_copy(state, here, sems.at[i])
        for i, (state, here) in enumerate(zip(states, held))
    ]
    for copy in copies:
        copy.start()
    sums[...] = jnp.zeros(sums.shape, F32)
    for f in range(got.shape[0]):
        sums[regions[f]] += got[f].astype(F32)
    for copy in copies:
        copy.wait()
    param, moment, second = held
    rows = param.shape[2]
    for side in range(2):
        for r in range(param.shape[1]):
            p, m, v = adamw_values(
                param[side, r], moment[side, r], second[side, r], sums[r, side],
                fixes[0], fixes[1],
            )
            new_param[side, r] = p
            new_moment[side, r] = m
            new_second[side, r] = v
            rounded[pl.ds((side * param.shape[1] + r) * rows, rows), :] = p.astype(BF16)


def adapter_update(regions, fixes, got, param, moment, second):
    hbm = pl.BlockSpec(memory_space=pltpu.HBM)
    vmem = pl.BlockSpec(memory_space=pltpu.VMEM)
    smem = pl.BlockSpec(memory_space=pltpu.SMEM)
    like = jax.ShapeDtypeStruct(param.shape, F32)
    rounded = jax.ShapeDtypeStruct((math.prod(param.shape[:3]), param.shape[3]), BF16)
    return pl.pallas_call(
        adapter_kernel,
        out_shape=(like, like, like, rounded),
        in_specs=[smem, smem, vmem, hbm, hbm, hbm],
        out_specs=(vmem,) * 4,
        scratch_shapes=[pltpu.VMEM(param.shape, F32)] * 3
        + [
            pltpu.VMEM((param.shape[1],) + got.shape[1:], F32),
            pltpu.SemaphoreType.DMA((3,)),
        ],
        compiler_params=pltpu.CompilerParams(vmem_limit_bytes=16 * 1024 * 1024),
    )(regions, fixes, got, param, moment, second)


def pick_kernel(where, *refs):
    arrays, outs = refs[:4], refs[4:]
    wide = outs[0].shape[0]
    for k, out in enumerate(outs):
        row_y = 2 * (where[ZL] ^ (k % 2)) + ((where[X] & 1) ^ (k // 2))
        away = (row_y - where[Y] + 4) & 3
        place = away ^ (away >> 1)
        rows = pl.ds(pl.multiple_of(place * wide, wide), wide)
        total = arrays[0][rows, :].astype(F32)
        for array in arrays[1:]:
            total = total + array[rows, :].astype(F32)
        out[...] = total.astype(BF16)


def pick_blocks(here, arrays):
    vmem = pl.BlockSpec(memory_space=pltpu.VMEM)
    rows, columns = arrays[0].shape
    return pl.pallas_call(
        pick_kernel,
        out_shape=(jax.ShapeDtypeStruct((rows // 4, columns), BF16),) * 4,
        in_specs=[pl.BlockSpec(memory_space=pltpu.SMEM)] + [vmem] * 4,
        out_specs=(vmem,) * 4,
        compiler_params=pltpu.CompilerParams(vmem_limit_bytes=32 * 1024 * 1024),
    )(here, *arrays)


def weight_kernel(scale, where, fixes, *refs):
    terms, (param, moment, second, extra), outs = refs[:4], refs[4:8], refs[8:]
    new_param, new_moment, new_second, rounded = outs
    rows, wide = terms[0].shape
    for ka in range(2):
        grad = terms[2 * ka][...].astype(F32) + terms[2 * ka + 1][...].astype(F32)
        grad = grad * scale
        for h in range(2):

            @pl.when(((where[X] >> 1) ^ ka) == h)
            def _():
                columns = pl.ds(h * wide, wide)
                p, m, v = adamw_values(
                    param[:, columns], moment[:, columns], second[:, columns], grad,
                    fixes[0], fixes[1],
                )
                new_param[:, columns] = p
                new_moment[:, columns] = m
                new_second[:, columns] = v
                rounded[pl.ds(h * rows, rows), :] = p.astype(BF16)

    rounded[pl.ds(2 * rows, extra.shape[0]), :] = extra[...]


def weight_update(here, scale, fixes, terms, param, moment, second, extra):
    vmem = pl.BlockSpec(memory_space=pltpu.VMEM)
    smem = pl.BlockSpec(memory_space=pltpu.SMEM)
    like = jax.ShapeDtypeStruct(param.shape, F32)
    rounded = jax.ShapeDtypeStruct((2 * param.shape[0] + extra.shape[0], extra.shape[1]), BF16)
    return pl.pallas_call(
        functools.partial(weight_kernel, scale),
        out_shape=(like, like, like, rounded),
        in_specs=[smem, smem] + [vmem] * 8,
        out_specs=(vmem,) * 4,
        compiler_params=pltpu.CompilerParams(vmem_limit_bytes=32 * 1024 * 1024),
    )(here, fixes, *terms, param, moment, second, extra)


def place_kernel(slots, where, own, peer, *refs):
    weight, adapter = refs[-2:]
    rows, wide = weight.shape[1], weight.shape[2] // 2
    for core, source in ((where[CORE], own), (1 - where[CORE], peer)):
        block = source[pl.program_id(0)]
        weight[core, :, :wide] = block[:rows]
        weight[core, :, wide:] = block[rows : 2 * rows]
        adapter[:, core] = block[2 * rows :].reshape(adapter.shape[0:1] + adapter.shape[2:])


def place_blocks(here, slots, own, peer, rows, groups, outs):
    wide = own.shape[2]
    deep = (own.shape[1] - 2 * rows) // groups

    def chip(i, where):
        dx, dz = (functools.reduce(lambda rest, s: jnp.where(i == s[0], s[1], rest), enumerate(axis), 0) for axis in zip(*slots))
        return ((where[ZL] ^ dz) << 2) + ((where[X] + dx) & 3)

    def block(i, where):
        return (0, 0, 0)

    shapes = (
        jax.ShapeDtypeStruct((16, rows, 2 * wide), BF16),
        jax.ShapeDtypeStruct((groups, 16, deep, wide), BF16),
    )
    return pl.pallas_call(
        functools.partial(place_kernel, slots),
        out_shape=shapes,
        grid_spec=pltpu.PrefetchScalarGridSpec(
            num_scalar_prefetch=1,
            grid=(len(slots),),
            in_specs=[pl.BlockSpec(own.shape, block), pl.BlockSpec(own.shape, block)]
            + [pl.BlockSpec(memory_space=pl.ANY)] * len(outs),
            out_specs=(
                pl.BlockSpec((2, rows, 2 * wide), lambda i, where: (chip(i, where), 0, 0)),
                pl.BlockSpec((groups, 2, deep, wide), lambda i, where: (0, chip(i, where), 0, 0)),
            ),
        ),
        input_output_aliases={3: 0, 4: 1} if outs else {},
        compiler_params=pltpu.CompilerParams(vmem_limit_bytes=24 * 1024 * 1024),
    )(here, own, peer, *outs)


def shards(
    activations,
    cotangent,
    step_count,
    region_of,
    weight_master,
    weight_moment,
    weight_second,
    adapter_copy,
    adapter_master,
    adapter_moment,
    adapter_second,
):
    fsdp_count = lax.axis_size("fsdp")
    tp_count = lax.axis_size("tp")
    tok_dev = activations.shape[0]
    width = activations.shape[1] * tp_count
    rank = adapter_copy.shape[3]
    region_count = adapter_copy.shape[1]
    grad_scale = math.sqrt(width / (tok_dev * fsdp_count))
    inv_width = 1.0 / math.sqrt(width)
    inv_rank = 1.0 / math.sqrt(rank)
    f = lax.axis_index("fsdp")
    t = lax.axis_index("tp")
    zl, x, c = f // 8, (f // 2) % 4, f % 2
    y, zh = t // 2, t % 2

    here = jnp.stack([x, y, zl, zh, c, f]).astype(jnp.int32)
    step_float = step_count[0].astype(F32)
    fixes = jnp.stack([
        1.0 - jnp.power(F32(beta_first), step_float),
        1.0 - jnp.power(F32(beta_second), step_float),
    ])

    low_keep, low_give = low_parts(
        here, region_of, activations, cotangent, adapter_copy, (inv_width, inv_rank)
    )
    low_got = move(low_give, other_zh)

    middle = tok_dev // 2
    back = move(activations, along_y(1))
    ahead = move(activations, along_y(-1))
    low_got, cot_give, back_half, ahead_half = lax.optimization_barrier(
        (low_got, cotangent, back[:middle], ahead[middle:])
    )
    cot_zh = move(cot_give, other_zh)
    far_first = move(back_half, along_y(1))
    far_second = move(ahead_half, along_y(-1))

    low = low_add(low_keep, low_got).reshape(4, tok_dev // 8, 2 * rank)
    low_sum = sum_parts(swap_among(low, "tp", Y_GROUPS))

    def swapped(acts, cot):
        keep, give = partials(here, acts, cot)
        return [keep, move(give, other_core)]

    low_sum, back, ahead, far_first, far_second = lax.optimization_barrier(
        (low_sum, back, ahead, far_first, far_second)
    )
    low_both = jnp.stack([low_sum, move(low_sum, other_zh)])
    near_acts, far_acts = [[activations], [ahead], [back]], [[far_first, far_second]]
    parts = swapped(near_acts, cotangent) + swapped(far_acts, cotangent)
    parts += swapped(near_acts, cot_zh) + swapped(far_acts, cot_zh)
    blocks = add_blocks(here, parts)
    low_pieces = [low_both] + [move(low_both, along_y(k)) for k in (1, 2, 3)]
    blocks = [blocks[0]] + [move(blocks[k], along_x(k)) for k in (3, 1, 2)]
    blocks = pick_blocks(here, blocks)

    parts = adapter_grads(
        here, low_pieces, activations, cotangent,
        (inv_width * grad_scale, inv_rank * grad_scale), fsdp_count,
    )
    got = lax.all_to_all(parts, "fsdp", 0, 0)
    new_adapter, new_adapter_moment, new_adapter_second, adapter_rows = adapter_update(
        region_of, fixes, got, adapter_master, adapter_moment, adapter_second
    )
    terms = [move(block, to_owner(k // 2, k % 2)) for k, block in enumerate(blocks)]
    new_weight, new_weight_moment, new_weight_second, piece = weight_update(
        here, inv_width * grad_scale, fixes, terms, weight_master, weight_moment, weight_second, adapter_rows
    )

    from_zl = move(piece, other_zl)
    from_ahead = move(piece, along_x(-1))
    from_back = move(piece, along_x(1))
    from_far = move(piece, along_x(2))
    first = jnp.stack([piece, from_zl, from_back, from_ahead])
    second = jnp.stack([
        from_far,
        move(from_zl, along_x(1)),
        move(from_zl, along_x(-1)),
        move(from_far, other_zl),
    ])

    outs = ()
    for slots, blocks in (
        (((0, 0), (0, 1), (-1, 0), (1, 0)), first),
        (((2, 0), (-1, 1), (1, 1), (2, 1)), second),
    ):
        outs = place_blocks(
            here, slots, blocks, move(blocks, other_core), new_weight.shape[0],
            2 * region_count, outs,
        )
    weight_next = outs[0].reshape(width, -1)
    adapter_next = outs[1].reshape(adapter_copy.shape)
    return (
        new_weight,
        new_weight_moment,
        new_weight_second,
        weight_next,
        new_adapter,
        new_adapter_moment,
        new_adapter_second,
        adapter_next,
    )


def solution(mesh):
    return jax.shard_map(
        shards,
        mesh=mesh,
        in_specs=(
            P("fsdp", "tp"),
            P("fsdp", "tp"),
            P(),
            P(),
            P("fsdp", "tp"),
            P("fsdp", "tp"),
            P("fsdp", "tp"),
            P(None, None, "tp", None),
            P(None, None, ("tp", "fsdp"), None),
            P(None, None, ("tp", "fsdp"), None),
            P(None, None, ("tp", "fsdp"), None),
        ),
        out_specs=(
            P("fsdp", "tp"),
            P("fsdp", "tp"),
            P("fsdp", "tp"),
            P(None, "tp"),
            P(None, None, ("tp", "fsdp"), None),
            P(None, None, ("tp", "fsdp"), None),
            P(None, None, ("tp", "fsdp"), None),
            P(None, None, "tp", None),
        ),
        check_vma=False,
    )
```

```python
import functools
import math

import jax
import jax.numpy as jnp
from jax import lax
from jax.experimental import pallas as pl
from jax.experimental.pallas import tpu as pltpu
from jax.sharding import PartitionSpec as P

beta_first = 0.9
beta_second = 0.95
adam_eps = 1e-08
learn_rate = 0.1
decay_rate = 0.1

AXES = ("fsdp", "tp")
X, Y, ZL, ZH, CORE, FSDP = range(6)
F32 = jnp.float32
BF16 = jnp.bfloat16


def contract_rows(left, right):
    return lax.dot_general(
        left, right, (((0,), (0,)), ((), ())), preferred_element_type=jnp.float32
    )


def device_number(x, y, zl, zh, c):
    return (zl * 8 + x * 2 + c) * 8 + (y * 2 + zh)


def move(array, where):
    pairs = []
    for x in range(4):
        for y in range(4):
            for zl in range(2):
                for zh in range(2):
                    for c in range(2):
                        a, b, d, e, g = where(x, y, zl, zh, c)
                        pairs.append(
                            (device_number(x, y, zl, zh, c), device_number(a % 4, b % 4, d, e, g))
                        )
    return lax.ppermute(array, AXES, pairs)


def swap_among(array, axis, groups):
    return lax.all_to_all(array, axis, 0, 0, axis_index_groups=groups)


X_GROUPS = [[z * 8 + x * 2 + c for x in range(4)] for z in range(2) for c in range(2)]
ZL_X_GROUPS = [[z * 8 + x * 2 + c for z in range(2) for x in range(4)] for c in range(2)]
Y_GROUPS = [[y * 2 + z for y in range(4)] for z in range(2)]


def along_x(k):
    return lambda x, y, zl, zh, c: (x + k, y, zl, zh, c)


def along_y(k):
    return lambda x, y, zl, zh, c: (x, y + k, zl, zh, c)


def other_core(x, y, zl, zh, c):
    return (x, y, zl, zh, 1 - c)


def other_zl(x, y, zl, zh, c):
    return (x, y, 1 - zl, zh, c)


def other_zh(x, y, zl, zh, c):
    return (x, y, zl, 1 - zh, c)


def to_owner(ka, kb):
    return lambda x, y, zl, zh, c: (2 * ((x & 1) ^ ka) + zh, y, zl ^ kb, x >> 1, c)


def partials_kernel(counts, where, *refs):
    acts, (cot, keep, give) = refs[: sum(counts)], refs[-3:]
    c, wide = where[CORE], keep.shape[2]
    for out, h in ((keep, c), (give, 1 - c)):
        half = pl.ds(pl.multiple_of(h * wide, wide), wide)
        first = 0
        for d, count in enumerate(counts):
            for j in range(2):
                total, row = None, 0
                for ref in acts[first : first + count]:
                    block = cot[pl.ds(row, ref.shape[0]), pl.ds(j * wide, wide)]
                    term = contract_rows(ref[:, half], block)
                    total = term if total is None else total + term
                    row += ref.shape[0]
                out[j, pl.ds(d * wide, wide), :] = total.astype(BF16)
            first += count


def partials(here, acts, cot):
    counts = [len(parts) for parts in acts]
    flat = [part for parts in acts for part in parts]
    wide = flat[0].shape[1] // 2
    shape = (2, len(counts) * wide, wide)
    return pl.pallas_call(
        functools.partial(partials_kernel, counts),
        out_shape=(jax.ShapeDtypeStruct(shape, BF16),) * 2,
        in_specs=[pl.BlockSpec(memory_space=pltpu.SMEM)]
        + [pl.BlockSpec(memory_space=pltpu.VMEM)] * (len(flat) + 1),
        out_specs=(pl.BlockSpec(memory_space=pltpu.VMEM), pl.BlockSpec(memory_space=pltpu.VMEM)),
        compiler_params=pltpu.CompilerParams(vmem_limit_bytes=48 * 1024 * 1024),
    )(here, *flat, cot)


def add_kernel(where, *refs):
    parts, outs = refs[:8], refs[8:]
    rows = parts[0].shape[1]
    for k, out in enumerate(outs):
        quarter = (where[X] + k) & 3
        side, j = (quarter >> 1) ^ where[ZH], quarter & 1
        for number in range(2):

            @pl.when(side == number)
            def _():
                keep, got, keep_far, got_far = parts[4 * number : 4 * number + 4]
                out[:rows] = (keep[j].astype(F32) + got[j].astype(F32)).astype(BF16)
                out[rows:] = (keep_far[j].astype(F32) + got_far[j].astype(F32)).astype(BF16)


def add_blocks(here, parts):
    vmem = pl.BlockSpec(memory_space=pltpu.VMEM)
    _, rows, wide = parts[0].shape
    return pl.pallas_call(
        add_kernel,
        out_shape=(jax.ShapeDtypeStruct((rows + parts[2].shape[1], wide), BF16),) * 4,
        in_specs=[pl.BlockSpec(memory_space=pltpu.SMEM)] + [vmem] * 8,
        out_specs=(vmem,) * 4,
        compiler_params=pltpu.CompilerParams(vmem_limit_bytes=32 * 1024 * 1024),
    )(here, *parts)


def low_kernel(scales, where, regions, act, cot, adapters, keep, give, acts, cots, own, sems):
    rows, rank = keep.shape[0], own.shape[2]
    region = regions[where[FSDP]]
    copies = [
        pltpu.make_async_copy(adapters.at[0, region], own.at[0], sems.at[0]),
        pltpu.make_async_copy(act, acts, sems.at[1]),
        pltpu.make_async_copy(adapters.at[1, region], own.at[1], sems.at[2]),
        pltpu.make_async_copy(cot, cots, sems.at[3]),
    ]
    for copy in copies:
        copy.start()
    for side, source in enumerate((acts, cots)):
        copies[2 * side].wait()
        copies[2 * side + 1].wait()
        columns = pl.ds(side * rank, rank)
        for out, h in ((keep, where[ZH]), (give, 1 - where[ZH])):
            part = source[pl.ds(pl.multiple_of(h * rows, rows), rows), :]
            total = jnp.dot(part, own[side], preferred_element_type=F32) * scales[side]
            out[:, columns] = total.astype(out.dtype)


def low_parts(here, regions, act, cot, adapters, scales):
    rows, rank = act.shape[0] // 2, adapters.shape[3]
    smem = pl.BlockSpec(memory_space=pltpu.SMEM)
    hbm = pl.BlockSpec(memory_space=pltpu.HBM)
    vmem = pl.BlockSpec(memory_space=pltpu.VMEM)
    return pl.pallas_call(
        functools.partial(low_kernel, scales),
        out_shape=(
            jax.ShapeDtypeStruct((rows, 2 * rank), F32),
            jax.ShapeDtypeStruct((rows, 2 * rank), BF16),
        ),
        in_specs=[smem, smem, hbm, hbm, hbm],
        out_specs=(vmem, vmem),
        scratch_shapes=[
            pltpu.VMEM(act.shape, BF16),
            pltpu.VMEM(cot.shape, BF16),
            pltpu.VMEM((2,) + adapters.shape[2:], BF16),
            pltpu.SemaphoreType.DMA((4,)),
        ],
        compiler_params=pltpu.CompilerParams(vmem_limit_bytes=24 * 1024 * 1024),
    )(here, regions, act, cot, adapters)


def low_add_kernel(keep, got, out):
    out[...] = (keep[...] + got[...].astype(F32)).astype(BF16)


def low_add(keep, got):
    vmem = pl.BlockSpec(memory_space=pltpu.VMEM)
    return pl.pallas_call(
        low_add_kernel,
        out_shape=jax.ShapeDtypeStruct(keep.shape, BF16),
        in_specs=[vmem, vmem],
        out_specs=vmem,
        compiler_params=pltpu.CompilerParams(vmem_limit_bytes=16 * 1024 * 1024),
    )(keep, got)


def sum_kernel(parts, out):
    total = parts[0].astype(F32)
    for i in range(1, parts.shape[0]):
        total = total + parts[i].astype(F32)
    out[...] = total.astype(BF16)


def sum_parts(parts):
    vmem = pl.BlockSpec(memory_space=pltpu.VMEM)
    return pl.pallas_call(
        sum_kernel,
        out_shape=jax.ShapeDtypeStruct(parts.shape[1:], BF16),
        in_specs=[vmem],
        out_specs=vmem,
        compiler_params=pltpu.CompilerParams(vmem_limit_bytes=16 * 1024 * 1024),
    )(parts)


def grads_kernel(scales, where, *refs):
    pieces, (act, cot, out, low) = refs[:4], refs[4:]
    rows, rank = pieces[0].shape[1], out.shape[3]
    for k, piece in enumerate(pieces):
        for other in range(2):
            place = 4 * (where[ZH] ^ other) + ((where[Y] - k + 4) & 3)
            low[pl.ds(pl.multiple_of(place * rows, rows), rows), :] = piece[other]
    for side, source, start in ((0, act, rank), (1, cot, 0)):
        total = contract_rows(source[...], low[:, pl.ds(start, rank)])
        total = (total * scales[side]).astype(BF16)
        for f in range(out.shape[0]):
            out[f, side] = total[f * out.shape[2] : (f + 1) * out.shape[2]]


def adapter_grads(here, pieces, act, cot, scales, count):
    rank = pieces[0].shape[2] // 2
    vmem = pl.BlockSpec(memory_space=pltpu.VMEM)
    return pl.pallas_call(
        functools.partial(grads_kernel, scales),
        out_shape=jax.ShapeDtypeStruct((count, 2, act.shape[1] // count, rank), BF16),
        in_specs=[pl.BlockSpec(memory_space=pltpu.SMEM)] + [vmem] * 6,
        out_specs=vmem,
        scratch_shapes=[pltpu.VMEM((act.shape[0], 2 * rank), BF16)],
        compiler_params=pltpu.CompilerParams(vmem_limit_bytes=32 * 1024 * 1024),
    )(here, *pieces, act, cot)


def adamw_values(param, moment, second, grad, first_fix, second_fix):
    moment_new = beta_first * moment + (1.0 - beta_first) * grad
    second_new = beta_second * second + (1.0 - beta_second) * grad * grad
    ratio = moment_new / first_fix / (jnp.sqrt(second_new / second_fix) + adam_eps)
    return param - learn_rate * (ratio + decay_rate * param), moment_new, second_new


def adapter_kernel(regions, fixes, got, *refs):
    states, (new_param, new_moment, new_second, rounded), held, sums, sems = (
        refs[:3], refs[3:7], refs[7:10], refs[10], refs[11]
    )
    copies = [
        pltpu.make_async_copy(state, here, sems.at[i])
        for i, (state, here) in enumerate(zip(states, held))
    ]
    for copy in copies:
        copy.start()
    sums[...] = jnp.zeros(sums.shape, F32)
    for f in range(got.shape[0]):
        sums[regions[f]] += got[f].astype(F32)
    for copy in copies:
        copy.wait()
    param, moment, second = held
    rows = param.shape[2]
    for side in range(2):
        for r in range(param.shape[1]):
            p, m, v = adamw_values(
                param[side, r], moment[side, r], second[side, r], sums[r, side],
                fixes[0], fixes[1],
            )
            new_param[side, r] = p
            new_moment[side, r] = m
            new_second[side, r] = v
            rounded[pl.ds((side * param.shape[1] + r) * rows, rows), :] = p.astype(BF16)


def adapter_update(regions, fixes, got, param, moment, second):
    hbm = pl.BlockSpec(memory_space=pltpu.HBM)
    vmem = pl.BlockSpec(memory_space=pltpu.VMEM)
    smem = pl.BlockSpec(memory_space=pltpu.SMEM)
    like = jax.ShapeDtypeStruct(param.shape, F32)
    rounded = jax.ShapeDtypeStruct((math.prod(param.shape[:3]), param.shape[3]), BF16)
    return pl.pallas_call(
        adapter_kernel,
        out_shape=(like, like, like, rounded),
        in_specs=[smem, smem, vmem, hbm, hbm, hbm],
        out_specs=(vmem,) * 4,
        scratch_shapes=[pltpu.VMEM(param.shape, F32)] * 3
        + [
            pltpu.VMEM((param.shape[1],) + got.shape[1:], F32),
            pltpu.SemaphoreType.DMA((3,)),
        ],
        compiler_params=pltpu.CompilerParams(vmem_limit_bytes=16 * 1024 * 1024),
    )(regions, fixes, got, param, moment, second)


def pick_kernel(where, *refs):
    arrays, outs = refs[:4], refs[4:]
    wide = outs[0].shape[0]
    for k, out in enumerate(outs):
        row_y = 2 * (where[ZL] ^ (k % 2)) + ((where[X] & 1) ^ (k // 2))
        away = (row_y - where[Y] + 4) & 3
        place = away ^ (away >> 1)
        rows = pl.ds(pl.multiple_of(place * wide, wide), wide)
        total = arrays[0][rows, :].astype(F32)
        for array in arrays[1:]:
            total = total + array[rows, :].astype(F32)
        out[...] = total.astype(BF16)


def pick_blocks(here, arrays):
    vmem = pl.BlockSpec(memory_space=pltpu.VMEM)
    rows, columns = arrays[0].shape
    return pl.pallas_call(
        pick_kernel,
        out_shape=(jax.ShapeDtypeStruct((rows // 4, columns), BF16),) * 4,
        in_specs=[pl.BlockSpec(memory_space=pltpu.SMEM)] + [vmem] * 4,
        out_specs=(vmem,) * 4,
        compiler_params=pltpu.CompilerParams(vmem_limit_bytes=32 * 1024 * 1024),
    )(here, *arrays)


def weight_kernel(scale, where, fixes, *refs):
    terms, (param, moment, second, extra), outs = refs[:4], refs[4:8], refs[8:]
    new_param, new_moment, new_second, rounded = outs
    rows, wide = terms[0].shape
    for ka in range(2):
        grad = terms[2 * ka][...].astype(F32) + terms[2 * ka + 1][...].astype(F32)
        grad = grad * scale
        for h in range(2):

            @pl.when(((where[X] >> 1) ^ ka) == h)
            def _():
                columns = pl.ds(h * wide, wide)
                p, m, v = adamw_values(
                    param[:, columns], moment[:, columns], second[:, columns], grad,
                    fixes[0], fixes[1],
                )
                new_param[:, columns] = p
                new_moment[:, columns] = m
                new_second[:, columns] = v
                rounded[pl.ds(h * rows, rows), :] = p.astype(BF16)

    rounded[pl.ds(2 * rows, extra.shape[0]), :] = extra[...]


def weight_update(here, scale, fixes, terms, param, moment, second, extra):
    vmem = pl.BlockSpec(memory_space=pltpu.VMEM)
    smem = pl.BlockSpec(memory_space=pltpu.SMEM)
    like = jax.ShapeDtypeStruct(param.shape, F32)
    rounded = jax.ShapeDtypeStruct((2 * param.shape[0] + extra.shape[0], extra.shape[1]), BF16)
    return pl.pallas_call(
        functools.partial(weight_kernel, scale),
        out_shape=(like, like, like, rounded),
        in_specs=[smem, smem] + [vmem] * 8,
        out_specs=(vmem,) * 4,
        compiler_params=pltpu.CompilerParams(vmem_limit_bytes=32 * 1024 * 1024),
    )(here, fixes, *terms, param, moment, second, extra)


def place_kernel(slots, where, own, peer, *refs):
    weight, adapter = refs[-2:]
    rows, wide = weight.shape[1], weight.shape[2] // 2
    for core, source in ((where[CORE], own), (1 - where[CORE], peer)):
        block = source[pl.program_id(0)]
        weight[core, :, :wide] = block[:rows]
        weight[core, :, wide:] = block[rows : 2 * rows]
        adapter[:, core] = block[2 * rows :].reshape(adapter.shape[0:1] + adapter.shape[2:])


def place_blocks(here, slots, own, peer, rows, groups, outs):
    wide = own.shape[2]
    deep = (own.shape[1] - 2 * rows) // groups

    def chip(i, where):
        dx, dz = (functools.reduce(lambda rest, s: jnp.where(i == s[0], s[1], rest), enumerate(axis), 0) for axis in zip(*slots))
        return ((where[ZL] ^ dz) << 2) + ((where[X] + dx) & 3)

    def block(i, where):
        return (0, 0, 0)

    shapes = (
        jax.ShapeDtypeStruct((16, rows, 2 * wide), BF16),
        jax.ShapeDtypeStruct((groups, 16, deep, wide), BF16),
    )
    return pl.pallas_call(
        functools.partial(place_kernel, slots),
        out_shape=shapes,
        grid_spec=pltpu.PrefetchScalarGridSpec(
            num_scalar_prefetch=1,
            grid=(len(slots),),
            in_specs=[pl.BlockSpec(own.shape, block), pl.BlockSpec(own.shape, block)]
            + [pl.BlockSpec(memory_space=pl.ANY)] * len(outs),
            out_specs=(
                pl.BlockSpec((2, rows, 2 * wide), lambda i, where: (chip(i, where), 0, 0)),
                pl.BlockSpec((groups, 2, deep, wide), lambda i, where: (0, chip(i, where), 0, 0)),
            ),
        ),
        input_output_aliases={3: 0, 4: 1} if outs else {},
        compiler_params=pltpu.CompilerParams(vmem_limit_bytes=24 * 1024 * 1024),
    )(here, own, peer, *outs)


def shards(
    activations,
    cotangent,
    step_count,
    region_of,
    weight_master,
    weight_moment,
    weight_second,
    adapter_copy,
    adapter_master,
    adapter_moment,
    adapter_second,
):
    fsdp_count = lax.axis_size("fsdp")
    tp_count = lax.axis_size("tp")
    tok_dev = activations.shape[0]
    width = activations.shape[1] * tp_count
    rank = adapter_copy.shape[3]
    region_count = adapter_copy.shape[1]
    grad_scale = math.sqrt(width / (tok_dev * fsdp_count))
    inv_width = 1.0 / math.sqrt(width)
    inv_rank = 1.0 / math.sqrt(rank)
    f = lax.axis_index("fsdp")
    t = lax.axis_index("tp")
    zl, x, c = f // 8, (f // 2) % 4, f % 2
    y, zh = t // 2, t % 2

    here = jnp.stack([x, y, zl, zh, c, f]).astype(jnp.int32)
    step_float = step_count[0].astype(F32)
    fixes = jnp.stack([
        1.0 - jnp.power(F32(beta_first), step_float),
        1.0 - jnp.power(F32(beta_second), step_float),
    ])

    low_keep, low_give = low_parts(
        here, region_of, activations, cotangent, adapter_copy, (inv_width, inv_rank)
    )
    low_got = move(low_give, other_zh)

    middle = tok_dev // 2
    back = move(activations, along_y(1))
    ahead = move(activations, along_y(-1))
    low_got, cot_give, back_half, ahead_half = lax.optimization_barrier(
        (low_got, cotangent, back[:middle], ahead[middle:])
    )
    cot_zh = move(cot_give, other_zh)
    far_first = move(back_half, along_y(1))
    far_second = move(ahead_half, along_y(-1))

    low = low_add(low_keep, low_got).reshape(4, tok_dev // 8, 2 * rank)
    low_sum = sum_parts(swap_among(low, "tp", Y_GROUPS))

    def swapped(acts, cot):
        keep, give = partials(here, acts, cot)
        return [keep, move(give, other_core)]

    low_sum, back, ahead, far_first, far_second = lax.optimization_barrier(
        (low_sum, back, ahead, far_first, far_second)
    )
    low_both = jnp.stack([low_sum, move(low_sum, other_zh)])
    near_acts, far_acts = [[activations], [ahead], [back]], [[far_first, far_second]]
    parts = swapped(near_acts, cotangent) + swapped(far_acts, cotangent)
    parts += swapped(near_acts, cot_zh) + swapped(far_acts, cot_zh)
    blocks = add_blocks(here, parts)
    low_pieces = [low_both] + [move(low_both, along_y(k)) for k in (1, 2, 3)]
    blocks = [blocks[0]] + [move(blocks[k], along_x(k)) for k in (3, 1, 2)]
    blocks = pick_blocks(here, blocks)

    parts = adapter_grads(
        here, low_pieces, activations, cotangent,
        (inv_width * grad_scale, inv_rank * grad_scale), fsdp_count,
    )
    got = lax.all_to_all(parts, "fsdp", 0, 0)
    new_adapter, new_adapter_moment, new_adapter_second, adapter_rows = adapter_update(
        region_of, fixes, got, adapter_master, adapter_moment, adapter_second
    )
    terms = [move(block, to_owner(k // 2, k % 2)) for k, block in enumerate(blocks)]
    new_weight, new_weight_moment, new_weight_second, piece = weight_update(
        here, inv_width * grad_scale, fixes, terms, weight_master, weight_moment, weight_second, adapter_rows
    )

    from_zl = move(piece, other_zl)
    from_ahead = move(piece, along_x(-1))
    from_back = move(piece, along_x(1))
    from_far = move(piece, along_x(2))
    first = jnp.stack([piece, from_zl, from_back, from_ahead])
    zl_ahead = move(from_zl, along_x(-1))
    zl_back = move(from_zl, along_x(1))
    second = jnp.stack([from_far, zl_back, zl_ahead, move(from_far, other_zl)])

    outs = ()
    for slots, blocks in (
        (((0, 0), (0, 1), (-1, 0), (1, 0)), first),
        (((2, 0), (-1, 1), (1, 1), (2, 1)), second),
    ):
        outs = place_blocks(
            here, slots, blocks, move(blocks, other_core), new_weight.shape[0],
            2 * region_count, outs,
        )
    weight_next = outs[0].reshape(width, -1)
    adapter_next = outs[1].reshape(adapter_copy.shape)
    return (
        new_weight,
        new_weight_moment,
        new_weight_second,
        weight_next,
        new_adapter,
        new_adapter_moment,
        new_adapter_second,
        adapter_next,
    )


def solution(mesh):
    return jax.shard_map(
        shards,
        mesh=mesh,
        in_specs=(
            P("fsdp", "tp"),
            P("fsdp", "tp"),
            P(),
            P(),
            P("fsdp", "tp"),
            P("fsdp", "tp"),
            P("fsdp", "tp"),
            P(None, None, "tp", None),
            P(None, None, ("tp", "fsdp"), None),
            P(None, None, ("tp", "fsdp"), None),
            P(None, None, ("tp", "fsdp"), None),
        ),
        out_specs=(
            P("fsdp", "tp"),
            P("fsdp", "tp"),
            P("fsdp", "tp"),
            P(None, "tp"),
            P(None, None, ("tp", "fsdp"), None),
            P(None, None, ("tp", "fsdp"), None),
            P(None, None, ("tp", "fsdp"), None),
            P(None, None, "tp", None),
        ),
        check_vma=False,
    )
```
